32 devices in a mesh: dp: 4 (over x, core), gx: 2 (over y), gy: 4 (over z).
Axes of the slice: x: 2, y: 2, z: 4, core: 2. Of those that a mesh axis runs over, the one named last changes fastest.
Arguments:
- hidden_in: bfloat16 [16384, 1024], P(('dp', 'gx'), 'gy'), may hold values from -15 to 15
- ln1_gain: float32 [1024], P('gy'), may hold values from 0.3 to 2
- ln1_bias: float32 [1024], P('gy'), may hold values from -3 to 3
- ln2_gain: float32 [1024], P('gy'), may hold values from 0.3 to 2
- ln2_bias: float32 [1024], P('gy'), may hold values from -3 to 3
- w_qkv: bfloat16 [1024, 3072], P('gy', 'gx'), may hold values from -0.1875 to 0.1875
- b_qkv: float32 [3072], P('gx'), may hold values from -3 to 3
- w_dense: bfloat16 [1024, 1024], P('gx', 'gy'), may hold values from -1 to 1
- b_dense: float32 [1024], P('gy'), may hold values from -3 to 3
- w_up: bfloat16 [1024, 4096], P('gy', 'gx'), may hold values from -0.1875 to 0.1875
- b_up: float32 [4096], P('gx'), may hold values from -3 to 3
- w_down: bfloat16 [4096, 1024], P('gx', 'gy'), may hold values from -0.09375 to 0.09375
- b_down: float32 [1024], P('gy'), may hold values from -3 to 3
- cotangent: bfloat16 [16384, 1024], P(('dp', 'gx'), 'gy'), may hold values from -6 to 6
Outputs:
- hidden_out: bfloat16 [16384, 1024], P(('dp', 'gx'), 'gy')
- grad_input: bfloat16 [16384, 1024], P(('dp', 'gx'), 'gy')
- grad_ln1_gain: float32 [1024], P('gy')
- grad_ln1_bias: float32 [1024], P('gy')
- grad_ln2_gain: float32 [1024], P('gy')
- grad_ln2_bias: float32 [1024], P('gy')
- grad_w_qkv: float32 [1024, 3072], P('gy', 'gx')
- grad_b_qkv: float32 [3072], P('gx')
- grad_w_dense: float32 [1024, 1024], P('gx', 'gy')
- grad_b_dense: float32 [1024], P('gy')
- grad_w_up: float32 [1024, 4096], P('gy', 'gx')
- grad_b_up: float32 [4096], P('gx')
- grad_w_down: float32 [4096, 1024], P('gx', 'gy')
- grad_b_down: float32 [1024], P('gy')
The draws below stay inside these ranges and needn't reach their ends.
All inputs are finite; a program needn't handle non-finite values.
Results may differ from the reference program's by a relative error of at most 0.012.
The reference program's roundings to bfloat16 on the way count: a program that leaves them out, or rounds other values in their place, can miss the bound.
Values may be sent and summed in bfloat16 or wider, within the bound.
No kernel may reach another device: no remote copies, remote signals or barrier semaphores. Data moves between devices by JAX's collectives and lax.ppermute only.
A program may use at most 256 MiB of HBM per device.

```python
import jax
import jax.numpy as jnp
from jax import lax

D = 1024
H = 16
HD = 64
FF = 4096
ROT = 16
LEN = 1024
SEQ_DP = 4
TOKENS = 16384
N_DP = 4


def draw_hidden_in(key, part):
    first_key, second_key = jax.random.split(key, 2)
    columns = jnp.arange(D).astype(jnp.float32) / D
    column_scale = 0.6 * 3.0 ** columns * jax.random.uniform(first_key, (D,), jnp.float32, 0.7, 1.3)
    base = jnp.clip(jax.random.normal(second_key, (TOKENS, D), jnp.float32), -6.0, 6.0) + 0.2
    return (base * column_scale[None, :]).astype(jnp.bfloat16)


def gain_draw(key, marker):
    inner_key = jax.random.fold_in(key, marker)
    columns = jnp.arange(D).astype(jnp.float32) / D
    rough = jax.random.uniform(inner_key, (D,), jnp.float32, 0.8, 1.2)
    return (0.5 + columns) * rough


def draw_ln1_gain(key, part):
    return gain_draw(key, 11)


def draw_ln2_gain(key, part):
    return gain_draw(key, 23)


def level_of(stream_key, extent, pieces, low, high):
    level, own = 1.0, jax.random.fold_in(stream_key, 6)
    for axis_at, parts in pieces:
        draws = jnp.exp(jax.random.uniform(jax.random.fold_in(own, axis_at), (parts,), jnp.float32, low / len(pieces), high / len(pieces)))
        level = level * jnp.repeat(draws, extent[axis_at] // parts).reshape([-1 if axis == axis_at else 1 for axis in range(len(extent))])
    return level


def gaussian(own_key, dims, width, limit, cuts=(), kind=jnp.bfloat16):
    entries = jax.random.normal(own_key, dims, jnp.float32) * width
    if len(cuts) > 0:
        entries = level_of(own_key, dims, cuts, -0.22, 0.18) * entries
    return jnp.clip(entries, min=-limit, max=limit).astype(kind)


def setup_inputs(seed: int = 0) -> dict:
    key_of = jax.random.split(jax.random.key(seed), 15)
    return {
        "hidden_in": draw_hidden_in(jax.random.fold_in(key_of[14], 71), 0),
        "ln1_gain": draw_ln1_gain(jax.random.fold_in(key_of[14], 71), 0),
        "ln1_bias": gaussian(key_of[2], (D,), 0.5, 3.0, ((0, 4),), jnp.float32),
        "ln2_gain": draw_ln2_gain(jax.random.fold_in(key_of[14], 71), 0),
        "ln2_bias": gaussian(key_of[4], (D,), 0.5, 3.0, ((0, 4),), jnp.float32),
        "w_qkv": gaussian(key_of[5], (D, 3 * D), D ** -0.5, 0.1875, ((0, 4), (1, 2))),
        "b_qkv": gaussian(key_of[6], (3 * D,), 0.5, 3.0, ((0, 2),), jnp.float32),
        "w_dense": gaussian(key_of[7], (D, D), (D // 32) ** -0.5, 1.0, ((0, 2), (1, 4))),
        "b_dense": gaussian(key_of[8], (D,), 0.5, 3.0, ((0, 4),), jnp.float32),
        "w_up": gaussian(key_of[9], (D, FF), D ** -0.5, 0.1875, ((0, 4), (1, 2))),
        "b_up": gaussian(key_of[10], (FF,), 0.5, 3.0, ((0, 2),), jnp.float32),
        "w_down": gaussian(key_of[11], (FF, D), FF ** -0.5, 0.09375, ((0, 2), (1, 4))),
        "b_down": gaussian(key_of[12], (D,), 0.5, 3.0, ((0, 4),), jnp.float32),
        "cotangent": gaussian(key_of[13], (TOKENS, D), 1.0, 6.0, ((0, 8), (1, 4))),
    }


@jax.custom_vjp
def low(v):
    return lax.optimization_barrier(v.astype(jnp.bfloat16)).astype(jnp.float32)

@jax.custom_vjp
def low_back(v):
    return v

def low_keep(v):
    return (low(v), None)

def low_pass(kept, grad):
    return (grad,)

def back_keep(v):
    return (v, None)

def back_low(kept, grad):
    return (low(grad),)
low.defvjp(low_keep, low_pass)
low_back.defvjp(back_keep, back_low)
eps_norm = 1e-05
highest = lax.Precision.HIGHEST

def product(left, right):
    return jnp.dot(left, right, precision=highest, preferred_element_type=jnp.float32)

def angles(token_count):
    places = (jnp.arange(token_count) % LEN).astype(jnp.float32)
    freqs = 10000.0 ** (-jnp.arange(ROT // 2).astype(jnp.float32) * 2.0 / ROT)
    turned = places[:, None] * freqs[None, :]
    return (jnp.cos(turned)[:, None, :], jnp.sin(turned)[:, None, :])

def rotate(vectors, cosine, sine_part):
    half_rot = ROT // 2
    first_half = vectors[..., :half_rot]
    second_half = vectors[..., half_rot:ROT]
    return jnp.concatenate([first_half * cosine - second_half * sine_part, second_half * cosine + first_half * sine_part, vectors[..., ROT:]], axis=-1)

def attend(queries, keys_seq, values_seq):
    scores = low_back(jnp.einsum('qhe,khe->hqk', queries, keys_seq, precision=highest) * HD ** (-0.5))
    places = jnp.arange(LEN)
    causal = places[:, None] >= places[None, :]
    weights = jax.nn.softmax(jnp.where(causal[None], scores, -1e+30), axis=-1)
    return jnp.einsum('hqk,khe->qhe', low(weights), values_seq, precision=highest)

def block_forward(inputs, ln1_gain, ln1_bias, ln2_gain, ln2_bias, w_qkv, b_qkv, w_dense, b_dense, w_up, b_up, w_down, b_down):
    token_count = inputs.shape[0]
    row_mean = lax.optimization_barrier(jnp.mean(inputs, axis=1, keepdims=True))
    variance = lax.optimization_barrier(jnp.mean(inputs * inputs, axis=1, keepdims=True)) - row_mean * row_mean
    normed = (inputs - row_mean) * lax.rsqrt(variance + eps_norm)
    attn_in = low(normed * ln1_gain + ln1_bias)
    mlp_in = low(normed * ln2_gain + ln2_bias)
    projected = low_back(product(attn_in, w_qkv) + b_qkv).reshape(token_count, H, 3, HD)
    cosine, sine_part = angles(token_count)
    queries = low(rotate(projected[:, :, 0], cosine, sine_part))
    keys_all = low(rotate(projected[:, :, 1], cosine, sine_part))
    values_all = low(projected[:, :, 2])

    def per_sequence(tensor):
        return tensor.reshape(token_count // LEN, LEN, H, HD)
    checked = jax.checkpoint(attend)

    def one_sequence(trio_seq):
        return checked(trio_seq[0], trio_seq[1], trio_seq[2])
    mixed = lax.map(one_sequence, (per_sequence(queries), per_sequence(keys_all), per_sequence(values_all)))
    heads_out = low(low_back(mixed.reshape(token_count, D)))
    pre_act = low_back(product(mlp_in, w_up) + b_up)
    act_out = low(jax.nn.gelu(pre_act, approximate=False))
    return inputs + product(heads_out, w_dense) + b_dense + product(act_out, w_down) + b_down

def reference(hidden_in, ln1_gain, ln1_bias, ln2_gain, ln2_bias, w_qkv, b_qkv, w_dense, b_dense, w_up, b_up, w_down, b_down, cotangent):
    weight_args = tuple((weight_arg.astype(jnp.float32) for weight_arg in (ln1_gain, ln1_bias, ln2_gain, ln2_bias, w_qkv, b_qkv, w_dense, b_dense, w_up, b_up, w_down, b_down)))
    group_rows = SEQ_DP * LEN
    inputs = hidden_in.astype(jnp.float32).reshape(N_DP, group_rows, D)
    grads_out = cotangent.astype(jnp.float32).reshape(N_DP, group_rows, D)

    def one_group(running, group_pair):
        outputs, pullback = jax.vjp(block_forward, group_pair[0], *weight_args)
        gradients = pullback(group_pair[1])
        running = tuple((total_sum + gradient for total_sum, gradient in zip(running, gradients[1:])))
        return (running, (outputs.astype(jnp.bfloat16), gradients[0].astype(jnp.bfloat16)))
    start_totals = tuple((jnp.zeros_like(weight_arg) for weight_arg in weight_args))
    running, (outputs, input_grads) = lax.scan(one_group, start_totals, (inputs, grads_out))
    return (outputs.reshape(TOKENS, D), input_grads.reshape(TOKENS, D), running[0], running[1], running[2], running[3], running[4], running[5], running[6], running[7], running[8], running[9], running[10], running[11])
```

```python
import functools

import jax
import jax.numpy as jnp
from jax import lax
from jax.experimental import pallas as pl
from jax.experimental.pallas import tpu as pltpu
from jax.sharding import PartitionSpec as P

HD = 64
ROT = 16
LEN = 1024
EPS = 1e-05
F32 = jnp.float32
BF16 = jnp.bfloat16


def mm(left, right):
    return jnp.dot(left, right, preferred_element_type=F32)


def mm_t(left, right):
    return lax.dot_general(left, right, (((1,), (1,)), ((), ())), preferred_element_type=F32)


def t_mm(left, right):
    return lax.dot_general(left, right, (((0,), (0,)), ((), ())), preferred_element_type=F32)


def swap(value, axis, step, count):
    return lax.ppermute(value, axis, [(i, i ^ step) for i in range(count)])


def xor_order(value, index, count):
    rest = value.shape[1:]
    bit = 1
    while bit < count:
        paired = value.reshape((count // (2 * bit), 2, bit) + rest)
        turned = paired[:, ::-1]
        value = jnp.where((index & bit) != 0, turned, paired).reshape((count,) + rest)
        bit *= 2
    return value


def rope_tables(width):
    places = jnp.arange(LEN).astype(F32)
    freqs = 10000.0 ** (-jnp.arange(ROT // 2).astype(F32) * 2.0 / ROT)
    turned = places[:, None] * freqs[None, :]
    cosine, sine = jnp.cos(turned), jnp.sin(turned)
    rest = HD - ROT
    zeros = jnp.zeros_like(sine)
    keep = jnp.concatenate([cosine, cosine, jnp.ones((LEN, rest), F32)], axis=1)
    from_up = jnp.concatenate([-sine, zeros, jnp.zeros((LEN, rest), F32)], axis=1)
    from_down = jnp.concatenate([zeros, sine, jnp.zeros((LEN, rest), F32)], axis=1)
    return tuple(jnp.tile(part, (1, width // HD)) for part in (keep, from_up, from_down))


def attention_kernel(
    width, x_ref, wq_ref, b_ref, g_ref, wd_ref, keep_ref, up_ref, down_ref,
    heads_ref, dqkv_ref, db_ref, q_s, k_s, v_s, g_s, kt_s, vt_s, dk_s, dv_s,
):
    heads = width // HD
    half = ROT // 2
    block = 256
    scale = HD ** (-0.5)
    b_row = b_ref[...]

    def turn(value, rows, sign):
        return (
            value * keep_ref[rows, :]
            + sign * (pltpu.roll(value, width - half, 1) * up_ref[rows, :])
            + sign * (pltpu.roll(value, half, 1) * down_ref[rows, :])
        )

    for part in range(LEN // block):
        rows = pl.ds(part * block, block)
        proj = mm(x_ref[rows, :], wq_ref[...]) + b_row
        q_s[rows, :] = turn(proj[:, :width], rows, 1.0).astype(BF16)
        key = turn(proj[:, width : 2 * width], rows, 1.0)
        value = proj[:, 2 * width :]
        k_s[rows, :] = key.astype(BF16)
        v_s[rows, :] = value.astype(BF16)
        kt_s[:, rows] = key.T.astype(BF16)
        vt_s[:, rows] = value.T.astype(BF16)
        g_s[rows, :] = mm(g_ref[rows, :], wd_ref[...]).astype(BF16)

    dk_s[...] = jnp.zeros_like(dk_s)
    dv_s[...] = jnp.zeros_like(dv_s)
    lane_head = lax.broadcasted_iota(jnp.int32, (block, width), 1) // HD
    key_at = lax.broadcasted_iota(jnp.int32, (block, block), 0)
    query_at = lax.broadcasted_iota(jnp.int32, (block, block), 1)
    seen = key_at <= query_at
    db_q = jnp.zeros((1, width), F32)
    for part in range(LEN // block):
        rows = pl.ds(part * block, block)
        span = (part + 1) * block
        q_block, g_block = q_s[rows, :], g_s[rows, :]
        outs, dqs = [], []
        dk_new, dv_new = None, None
        for head in range(heads):
            own = lane_head == head
            q_own = jnp.where(own, q_block, jnp.zeros_like(q_block))
            g_own = jnp.where(own, g_block, jnp.zeros_like(g_block))
            scores = mm_t(k_s[:span, :], q_own)
            last = jnp.where(seen, scores[span - block :, :], -1e30)
            scores = last if part == 0 else jnp.concatenate([scores[: span - block, :], last], axis=0)
            top = jnp.max(scores, axis=0, keepdims=True)
            exponent = jnp.exp((scores - top) * scale)
            weights = exponent * (1.0 / jnp.sum(exponent, axis=0, keepdims=True))
            low = weights.astype(BF16)
            dweights = mm_t(v_s[:span, :], g_own)
            inner = jnp.sum(weights * dweights, axis=0, keepdims=True)
            dscores = (weights * (dweights - inner)).astype(BF16)
            at = slice(head * HD, (head + 1) * HD)
            outs.append(mm(vt_s[at, :span], low))
            dqs.append(mm(kt_s[at, :span], dscores))
            dv_here, dk_here = mm(low, g_own), mm(dscores, q_own)
            dv_new = dv_here if dv_new is None else dv_new + dv_here
            dk_new = dk_here if dk_new is None else dk_new + dk_here
        dk_s[:span, :] += dk_new
        dv_s[:span, :] += dv_new
        heads_ref[rows, :] = jnp.concatenate(outs, axis=0).T.astype(BF16)
        dq = jnp.concatenate(dqs, axis=0).T * scale
        dq_low = turn(dq, rows, -1.0).astype(BF16)
        dqkv_ref[rows, :width] = dq_low
        db_q = db_q + jnp.sum(dq_low.astype(F32), axis=0, keepdims=True)
    db_k = jnp.zeros((1, width), F32)
    db_v = jnp.zeros((1, width), F32)
    for part in range(LEN // block):
        rows = pl.ds(part * block, block)
        dk_low = turn(dk_s[rows, :] * scale, rows, -1.0).astype(BF16)
        dv_low = dv_s[rows, :].astype(BF16)
        dqkv_ref[rows, width : 2 * width] = dk_low
        dqkv_ref[rows, 2 * width :] = dv_low
        db_k = db_k + jnp.sum(dk_low.astype(F32), axis=0, keepdims=True)
        db_v = db_v + jnp.sum(dv_low.astype(F32), axis=0, keepdims=True)
    db_ref[:, :width] = db_q
    db_ref[:, width : 2 * width] = db_k
    db_ref[:, 2 * width :] = db_v


def attention_fused(attn_in, w_qkv, b_qkv, grad, w_dense_t, tables):
    width = w_dense_t.shape[1]
    features = attn_in.shape[1]
    return pl.pallas_call(
        functools.partial(attention_kernel, width),
        out_shape=(
            jax.ShapeDtypeStruct((LEN, width), BF16),
            jax.ShapeDtypeStruct((LEN, 3 * width), BF16),
            jax.ShapeDtypeStruct((1, 3 * width), F32),
        ),
        in_specs=[pl.BlockSpec(memory_space=pltpu.VMEM)] * 8,
        out_specs=tuple([pl.BlockSpec(memory_space=pltpu.VMEM)] * 3),
        scratch_shapes=[
            pltpu.VMEM((LEN, width), BF16),
            pltpu.VMEM((LEN, width), BF16),
            pltpu.VMEM((LEN, width), BF16),
            pltpu.VMEM((LEN, width), BF16),
            pltpu.VMEM((width, LEN), BF16),
            pltpu.VMEM((width, LEN), BF16),
            pltpu.VMEM((LEN, width), F32),
            pltpu.VMEM((LEN, width), F32),
        ],
        compiler_params=pltpu.CompilerParams(vmem_limit_bytes=48 * 1024 * 1024),
        cost_estimate=pl.CostEstimate(
            flops=2 * LEN * features * 4 * width + 20 * LEN * LEN * width,
            bytes_accessed=4 * LEN * features + 20 * LEN * width,
            transcendentals=LEN * LEN * width // HD,
        ),
    )(attn_in, w_qkv, b_qkv.reshape(1, -1), grad, w_dense_t, *tables)


def attention_plain(attn_in, w_qkv, b_qkv, grad, w_dense_t, tables):
    width = w_dense_t.shape[1]
    heads = width // HD
    keep, up, down = tables
    half = ROT // 2

    def turn(value, sign):
        return value * keep + sign * (
            jnp.roll(value, -half, 1) * up + jnp.roll(value, half, 1) * down
        )

    def split(value):
        return value.reshape(LEN, heads, HD)

    def product(pattern, left, right):
        return jnp.einsum(pattern, left, right, preferred_element_type=F32)

    proj = mm(attn_in, w_qkv) + b_qkv
    query = split(turn(proj[:, :width], 1.0).astype(BF16))
    key = split(turn(proj[:, width : 2 * width], 1.0).astype(BF16))
    value = split(proj[:, 2 * width :].astype(BF16))
    grad_low = split(mm(grad, w_dense_t).astype(BF16))
    places = jnp.arange(LEN)
    scores = product("qhe,khe->hqk", query, key) * HD ** (-0.5)
    weights = jax.nn.softmax(jnp.where(places[:, None] >= places[None, :], scores, -1e30), axis=-1)
    low = weights.astype(BF16)
    mixed = product("hqk,khe->qhe", low, value).reshape(LEN, width).astype(BF16)
    dweights = product("qhe,khe->hqk", grad_low, value)
    inner = jnp.sum(weights * dweights, axis=-1, keepdims=True)
    dscores = (weights * (dweights - inner)).astype(BF16)
    dq = product("hqk,khe->qhe", dscores, key).reshape(LEN, width) * HD ** (-0.5)
    dk = product("hqk,qhe->khe", dscores, query).reshape(LEN, width) * HD ** (-0.5)
    dv = product("hqk,qhe->khe", low, grad_low).reshape(LEN, width)
    dqkv = jnp.concatenate([turn(dq, -1.0), turn(dk, -1.0), dv], axis=1).astype(BF16)
    return mixed, dqkv, jnp.sum(dqkv.astype(F32), axis=0, keepdims=True)


def normalize(hidden):
    inputs = hidden.astype(F32)
    mean = jnp.mean(inputs, axis=1, keepdims=True)
    square = jnp.mean(inputs * inputs, axis=1, keepdims=True)
    inv_std = lax.rsqrt(square - mean * mean + EPS)
    return (inputs - mean) * inv_std, inv_std


def feed_forward(mlp_in, w_up, b_up, grad, w_down_t):
    pre = mm(mlp_in, w_up) + b_up
    grad_act = mm(grad, w_down_t)
    phi = 0.5 * (1.0 + lax.erf(pre * (0.5 ** 0.5)))
    slope = phi + pre * (jnp.exp(-0.5 * pre * pre) * 0.3989422804014327)
    act = (pre * phi).astype(BF16)
    dpre = (slope * grad_act).astype(BF16)
    return act, dpre, jnp.sum(dpre.astype(F32), axis=0, keepdims=True)


def sequence_pass(hidden, grad, gains, chunks, reduce_chunk):
    normed, inv_std = normalize(hidden)
    attn_in = (normed * gains[0] + gains[1]).astype(BF16)
    mlp_in = (normed * gains[2] + gains[3]).astype(BF16)
    width = chunks[0][2].shape[1]
    fused = width % 128 == 0
    tables = rope_tables(width)
    branch = grad_attn = grad_mlp = None
    weight_grads, bias_grads = [], []

    def add(total, term):
        return term if total is None else total + term

    ffn, att = [], []
    for w_qkv, b_qkv, w_dense_t, w_up, b_up, w_down_t in chunks:
        act, dpre, db_up = feed_forward(mlp_in, w_up, b_up, grad, w_down_t)
        branch = add(branch, mm_t(act, w_down_t))
        grad_mlp = add(grad_mlp, mm_t(dpre, w_up))
        ffn.append((t_mm(mlp_in, dpre), t_mm(grad, act), db_up))
    for w_qkv, b_qkv, w_dense_t, w_up, b_up, w_down_t in chunks:
        attention = attention_fused if fused else attention_plain
        mixed, dqkv, db_qkv = attention(attn_in, w_qkv, b_qkv, grad, w_dense_t, tables)
        branch = add(branch, mm_t(mixed, w_dense_t))
        grad_attn = add(grad_attn, mm_t(dqkv, w_qkv))
        att.append((t_mm(attn_in, dqkv), t_mm(grad, mixed), db_qkv))
    ups = reduce_chunk([item[0] for item in ffn])
    downs = reduce_chunk([item[1] for item in ffn])
    qkvs = reduce_chunk([item[0] for item in att])
    denses = reduce_chunk([item[1] for item in att])
    db_up = jnp.concatenate([item[2] for item in ffn], axis=0)
    db_qkv = jnp.concatenate([item[2] for item in att], axis=0)
    sums = jnp.stack(
        [
            jnp.sum(grad_attn * normed, axis=0),
            jnp.sum(grad_attn, axis=0),
            jnp.sum(grad_mlp * normed, axis=0),
            jnp.sum(grad_mlp, axis=0),
            jnp.sum(grad.astype(F32), axis=0),
        ]
    )
    grad_normed = grad_attn * gains[0] + grad_mlp * gains[2]
    row_sums = jnp.stack([jnp.sum(grad_normed, axis=1), jnp.sum(grad_normed * normed, axis=1)], axis=0)
    return normed, inv_std, branch, grad_normed, row_sums, sums, (qkvs, denses, ups, downs), db_qkv, db_up


def by_part(weight, heads):
    rows = weight.shape[0]
    return weight.reshape(rows, heads, 3, HD).transpose(0, 2, 1, 3).reshape(rows, -1)


def by_head(weight, heads):
    rows = weight.shape[0]
    return weight.reshape(rows, 3, heads, HD).transpose(0, 2, 1, 3).reshape(rows, -1)


def local_box(
    hidden_in, ln1_gain, ln1_bias, ln2_gain, ln2_bias, w_qkv, b_qkv, w_dense, b_dense, w_up, b_up,
    w_down, b_down, cotangent,
):
    dp, gx, gy = lax.axis_index("dp"), lax.axis_index("gx"), lax.axis_index("gy")
    wide = hidden_in.shape[1]
    half = wide // 2
    lower = gx == 0
    aligned = (gy // 2) == gx
    odd = (gy % 2) == 1

    def rel_rows(value):
        return jnp.where(lower, value, jnp.roll(value, -half, axis=0))

    def gather_z(value):
        return jnp.concatenate([value] + [swap(value, "gy", k, 4) for k in (1, 2, 3)], axis=0)

    def to_half(value):
        value = value.reshape(2, LEN, wide)
        first, second = value[:, :, :half], value[:, :, half:]
        kept = jnp.where(lower, first, second)
        got = swap(jnp.where(lower, second, first), "gx", 1, 2)
        near = jnp.where(aligned, kept, got)
        far = jnp.where(aligned, got, kept)
        near = jnp.where(odd, near[::-1], near)
        far = jnp.where(odd, far[::-1], far)
        pieces = [near[0], near[1], far[0], far[1]]
        return [pieces[0]] + [swap(pieces[k], "gy", k, 4) for k in (1, 2, 3)]

    def whole_rows(mine):
        other = [swap(piece, "gx", 1, 2) for piece in mine]
        return jnp.concatenate([part for pair in zip(mine, other) for part in pair], axis=1)

    def from_half(pieces):
        got = [pieces[0]] + [swap(pieces[k], "gy", k, 4) for k in (1, 2, 3)]
        near, far = jnp.stack(got[:2]), jnp.stack(got[2:])
        own = jnp.where(aligned, near, far)
        gone = jnp.where(aligned, far, near)
        own = jnp.where(odd, own[::-1], own)
        gone = jnp.where(odd, gone[::-1], gone)
        back = swap(gone, "gx", 1, 2)
        first = jnp.where(lower, own, back)
        second = jnp.where(lower, back, own)
        return jnp.concatenate([first, second], axis=2).reshape(2 * LEN, wide)

    hidden_half = to_half(hidden_in)
    hidden = whole_rows(hidden_half)
    grad_half = to_half(cotangent)
    grad = whole_rows(grad_half)

    vectors = jnp.stack([ln1_gain, ln1_bias, ln2_gain, ln2_bias, b_dense + b_down])
    vectors = rel_rows(vectors.T).T
    vectors = jnp.concatenate([vectors] + [swap(vectors, "gy", k, 4) for k in (1, 2, 3)], axis=1)

    heads = w_qkv.shape[1] // (3 * HD) // 4

    def quarter(value):
        columns = value.shape[1] // 4
        return lax.dynamic_slice_in_dim(value, dp * columns, columns, 1)

    def spread(value):
        block = gather_z(rel_rows(value))
        core = swap(block, "dp", 1, 4)
        across = swap(block, "dp", 2, 4)
        return [block, core, across, swap(across, "dp", 1, 4)]

    w_qkv_c = spread(by_part(quarter(w_qkv), heads))
    w_up_c = spread(quarter(w_up))
    w_dense_c = spread(lax.dynamic_slice_in_dim(w_dense, dp * (w_dense.shape[0] // 4), w_dense.shape[0] // 4, 0).T)
    w_down_c = spread(lax.dynamic_slice_in_dim(w_down, dp * (w_down.shape[0] // 4), w_down.shape[0] // 4, 0).T)
    b_qkv_c = xor_order(by_part(b_qkv.reshape(4, -1), heads), dp, 4)
    b_up_c = xor_order(b_up.reshape(4, -1), dp, 4)
    chunks = [
        (w_qkv_c[k], b_qkv_c[k], w_dense_c[k], w_up_c[k], b_up_c[k], w_down_c[k]) for k in range(4)
    ]

    def reduce_chunk(grads):
        sum_far = grads[2] + swap(grads[3].astype(BF16), "dp", 1, 4).astype(F32)
        sum_near = grads[0] + swap(grads[1].astype(BF16), "dp", 1, 4).astype(F32)
        total = sum_near + swap(sum_far.astype(BF16), "dp", 2, 4).astype(F32)
        blocks = total.reshape(4, wide, -1)
        low = blocks.astype(BF16)
        mine = blocks[0]
        for k in (1, 2, 3):
            mine = mine + swap(low[k], "gy", k, 4).astype(F32)
        mine = rel_rows(mine.astype(BF16))
        across = swap(mine, "dp", 2, 4)
        quarters = jnp.stack([mine, swap(mine, "dp", 1, 4), across, swap(across, "dp", 1, 4)])
        return xor_order(quarters, dp, 4)

    normed, inv_std, branch, grad_normed, row_sums, sums, reduced, db_qkv, db_up = sequence_pass(
        hidden, grad, vectors, chunks, reduce_chunk
    )

    def halves(value, which):
        return [value[:, (2 * k + which) * half : (2 * k + which + 1) * half] for k in range(4)]

    sent = [swap(part.astype(BF16), "gx", 1, 2) for part in halves(branch, 1)]
    bias_half = halves(vectors[4:5], 0)
    out_half = [
        (hidden_half[k].astype(F32) + part + sent[k].astype(F32) + bias_half[k]).astype(BF16)
        for k, part in enumerate(halves(branch, 0))
    ]
    hidden_out = from_half(out_half)

    features = 4 * wide
    row_sums = row_sums + swap(row_sums, "gx", 1, 2)
    mean_total = row_sums[0][:, None] / features
    mean_cross = row_sums[1][:, None] / features
    sent = [swap(part.astype(BF16), "gx", 1, 2) for part in halves(grad_normed, 1)]
    normed_half = halves(normed, 0)
    in_half = [
        (
            grad_half[k].astype(F32)
            + inv_std * (part + sent[k].astype(F32) - mean_total - normed_half[k] * mean_cross)
        ).astype(BF16)
        for k, part in enumerate(halves(grad_normed, 0))
    ]
    grad_input = from_half(in_half)

    sums = sums * jnp.array([1.0, 1.0, 1.0, 1.0, 0.5], F32)[:, None]
    mine = sums[:, :wide]
    for k in (1, 2, 3):
        mine = mine + swap(sums[:, k * wide : (k + 1) * wide], "gy", k, 4)
    mine = rel_rows(mine.T).T
    mine = mine + swap(mine, "gx", 1, 2)
    db = jnp.concatenate([xor_order(by_head(db_qkv, heads), dp, 4).reshape(-1), xor_order(db_up, dp, 4).reshape(-1)])
    db = db + swap(db, "gy", 1, 4)
    db = db + swap(db, "gy", 2, 4)
    both = jnp.concatenate([mine.reshape(-1), db])
    both = both + swap(both, "dp", 1, 4)
    both = both + swap(both, "dp", 2, 4)
    mine = both[: 5 * wide].reshape(5, wide)
    columns = w_qkv.shape[1]
    grad_b_qkv = both[5 * wide : 5 * wide + columns]
    grad_b_up = both[5 * wide + columns :]

    qkvs, denses, ups, downs = reduced

    def joined(quarters):
        return quarters.transpose(1, 0, 2).reshape(wide, -1).astype(F32)

    grad_w_qkv = joined(by_head(qkvs.reshape(4 * wide, -1), heads).reshape(4, wide, -1))
    grad_w_up = joined(ups)
    grad_w_dense = denses.transpose(0, 2, 1).reshape(-1, wide).astype(F32)
    grad_w_down = downs.transpose(0, 2, 1).reshape(-1, wide).astype(F32)
    return (
        hidden_out, grad_input, mine[0], mine[1], mine[2], mine[3], grad_w_qkv, grad_b_qkv,
        grad_w_dense, mine[4], grad_w_up, grad_b_up, grad_w_down, mine[4],
    )


def local_any(
    gx_count, gy_count,
    hidden_in, ln1_gain, ln1_bias, ln2_gain, ln2_bias, w_qkv, b_qkv, w_dense, b_dense, w_up, b_up,
    w_down, b_down, cotangent,
):
    heads = w_qkv.shape[1] // (3 * HD)

    def to_sequence(value):
        rows = lax.all_gather(value, "gx", axis=0, tiled=True)
        return lax.all_to_all(rows, "gy", split_axis=0, concat_axis=1, tiled=True)

    def from_sequence(value):
        return lax.all_to_all(value, "gy", split_axis=1, concat_axis=0, tiled=True)

    def gather(value):
        return lax.all_gather(value, "gy", axis=0, tiled=True)

    hidden, grad = to_sequence(hidden_in), to_sequence(cotangent)
    vectors = jnp.stack([ln1_gain, ln1_bias, ln2_gain, ln2_bias])
    vectors = lax.all_gather(vectors, "gy", axis=1, tiled=True)
    chunk = (
        gather(by_part(w_qkv, heads)),
        by_part(b_qkv[None], heads)[0],
        gather(w_dense.T),
        gather(w_up),
        b_up,
        gather(w_down.T),
    )

    def reduce_chunk(grads):
        return lax.psum(lax.psum_scatter(grads[0], "gy", scatter_dimension=0, tiled=True), "dp")

    normed, inv_std, branch, grad_normed, row_sums, sums, reduced, db_qkv, db_up = sequence_pass(
        hidden, grad, vectors, [chunk], reduce_chunk
    )
    branch_rows = lax.psum_scatter(from_sequence(branch), "gx", scatter_dimension=0, tiled=True)
    hidden_out = (hidden_in.astype(F32) + branch_rows + b_dense + b_down).astype(BF16)
    features = normed.shape[1]
    row_sums = lax.psum(row_sums, "gx")
    grad_normed = grad_normed - (
        row_sums[0][:, None] / features + normed * (row_sums[1][:, None] / features)
    ) * (1.0 / gx_count)
    grad_rows = lax.psum_scatter(from_sequence(inv_std * grad_normed), "gx", scatter_dimension=0, tiled=True)
    grad_input = (cotangent.astype(F32) + grad_rows).astype(BF16)
    sums = lax.psum_scatter(sums, "gy", scatter_dimension=1, tiled=True)
    sums = lax.psum(sums * jnp.array([1.0] * 4 + [1.0 / gx_count], F32)[:, None], ("dp", "gx"))
    db_qkv, db_up = lax.psum((by_head(db_qkv, heads)[0], db_up[0]), ("dp", "gy"))
    qkvs, denses, ups, downs = reduced
    return (
        hidden_out, grad_input, sums[0], sums[1], sums[2], sums[3], by_head(qkvs, heads), db_qkv,
        denses.T, sums[4], ups, db_up, downs.T, sums[4],
    )


def solution(mesh):
    sizes = mesh.shape
    boxed = sizes["dp"] == 4 and sizes["gx"] == 2 and sizes["gy"] == 4
    rows, feature = P(("dp", "gx"), "gy"), P("gy")
    placed = (
        rows, feature, feature, feature, feature, P("gy", "gx"), P("gx"), P("gx", "gy"), feature,
        P("gy", "gx"), P("gx"), P("gx", "gy"), feature, rows,
    )
    return jax.shard_map(
        local_box if boxed else functools.partial(local_any, sizes["gx"], sizes["gy"]),
        mesh=mesh,
        in_specs=placed,
        out_specs=(rows, rows) + placed[1:5] + placed[5:13],
        check_vma=False,
    )
```

```python
import functools

import jax
import jax.numpy as jnp
from jax import lax
from jax.experimental import pallas as pl
from jax.experimental.pallas import tpu as pltpu
from jax.sharding import PartitionSpec as P

HD = 64
ROT = 16
LEN = 1024
EPS = 1e-05
F32 = jnp.float32
BF16 = jnp.bfloat16


def mm(left, right):
    return jnp.dot(left, right, preferred_element_type=F32)


def mm_t(left, right):
    return lax.dot_general(left, right, (((1,), (1,)), ((), ())), preferred_element_type=F32)


def t_mm(left, right):
    return lax.dot_general(left, right, (((0,), (0,)), ((), ())), preferred_element_type=F32)


def swap(value, axis, step, count):
    return lax.ppermute(value, axis, [(i, i ^ step) for i in range(count)])


def xor_order(value, index, count):
    rest = value.shape[1:]
    bit = 1
    while bit < count:
        paired = value.reshape((count // (2 * bit), 2, bit) + rest)
        turned = paired[:, ::-1]
        value = jnp.where((index & bit) != 0, turned, paired).reshape((count,) + rest)
        bit *= 2
    return value


def rope_tables(width):
    place = lax.broadcasted_iota(jnp.int32, (LEN, width), 0).astype(F32)
    lane = lax.broadcasted_iota(jnp.int32, (LEN, width), 1) % HD
    half = ROT // 2
    turned = place * 10000.0 ** (-(lane % half).astype(F32) * 2.0 / ROT)
    cosine, sine = jnp.cos(turned), jnp.sin(turned)
    keep = jnp.where(lane < ROT, cosine, 1.0)
    from_up = jnp.where(lane < half, -sine, 0.0)
    from_down = jnp.where((lane >= half) & (lane < ROT), sine, 0.0)
    return keep, from_up, from_down


def attention_kernel(
    width, x_ref, wq_ref, b_ref, g_ref, wd_ref, keep_ref, up_ref, down_ref,
    heads_ref, dqkv_ref, db_ref, q_s, k_s, v_s, g_s, kt_s, vt_s, dk_s, dv_s,
):
    heads = width // HD
    half = ROT // 2
    block = 256
    scale = HD ** (-0.5)
    b_row = b_ref[...]

    def turn(value, rows, sign):
        return (
            value * keep_ref[rows, :]
            + sign * (pltpu.roll(value, width - half, 1) * up_ref[rows, :])
            + sign * (pltpu.roll(value, half, 1) * down_ref[rows, :])
        )

    for part in range(LEN // block):
        rows = pl.ds(part * block, block)
        proj = mm(x_ref[rows, :], wq_ref[...]) + b_row
        q_s[rows, :] = turn(proj[:, :width], rows, 1.0).astype(BF16)
        key = turn(proj[:, width : 2 * width], rows, 1.0)
        value = proj[:, 2 * width :]
        k_s[rows, :] = key.astype(BF16)
        v_s[rows, :] = value.astype(BF16)
        kt_s[:, rows] = key.T.astype(BF16)
        vt_s[:, rows] = value.T.astype(BF16)
        g_s[rows, :] = mm(g_ref[rows, :], wd_ref[...]).astype(BF16)

    dk_s[...] = jnp.zeros_like(dk_s)
    dv_s[...] = jnp.zeros_like(dv_s)
    lane_head = lax.broadcasted_iota(jnp.int32, (block, width), 1) // HD
    key_at = lax.broadcasted_iota(jnp.int32, (block, block), 0)
    query_at = lax.broadcasted_iota(jnp.int32, (block, block), 1)
    seen = key_at <= query_at
    db_q = jnp.zeros((1, width), F32)
    for part in range(LEN // block):
        rows = pl.ds(part * block, block)
        span = (part + 1) * block
        q_block, g_block = q_s[rows, :], g_s[rows, :]
        outs, dqs = [], []
        dk_new, dv_new = None, None
        for head in range(heads):
            own = lane_head == head
            q_own = jnp.where(own, q_block, jnp.zeros_like(q_block))
            g_own = jnp.where(own, g_block, jnp.zeros_like(g_block))
            scores = mm_t(k_s[:span, :], q_own)
            last = jnp.where(seen, scores[span - block :, :], -1e30)
            scores = last if part == 0 else jnp.concatenate([scores[: span - block, :], last], axis=0)
            top = jnp.max(scores, axis=0, keepdims=True)
            exponent = jnp.exp((scores - top) * scale)
            weights = exponent * (1.0 / jnp.sum(exponent, axis=0, keepdims=True))
            low = weights.astype(BF16)
            dweights = mm_t(v_s[:span, :], g_own)
            inner = jnp.sum(weights * dweights, axis=0, keepdims=True)
            dscores = (weights * (dweights - inner)).astype(BF16)
            at = slice(head * HD, (head + 1) * HD)
            outs.append(mm(vt_s[at, :span], low))
            dqs.append(mm(kt_s[at, :span], dscores))
            dv_here, dk_here = mm(low, g_own), mm(dscores, q_own)
            dv_new = dv_here if dv_new is None else dv_new + dv_here
            dk_new = dk_here if dk_new is None else dk_new + dk_here
        dk_s[:span, :] += dk_new
        dv_s[:span, :] += dv_new
        heads_ref[rows, :] = jnp.concatenate(outs, axis=0).T.astype(BF16)
        dq = jnp.concatenate(dqs, axis=0).T * scale
        dq_low = turn(dq, rows, -1.0).astype(BF16)
        dqkv_ref[rows, :width] = dq_low
        db_q = db_q + jnp.sum(dq_low.astype(F32), axis=0, keepdims=True)
    db_k = jnp.zeros((1, width), F32)
    db_v = jnp.zeros((1, width), F32)
    for part in range(LEN // block):
        rows = pl.ds(part * block, block)
        dk_low = turn(dk_s[rows, :] * scale, rows, -1.0).astype(BF16)
        dv_low = dv_s[rows, :].astype(BF16)
        dqkv_ref[rows, width : 2 * width] = dk_low
        dqkv_ref[rows, 2 * width :] = dv_low
        db_k = db_k + jnp.sum(dk_low.astype(F32), axis=0, keepdims=True)
        db_v = db_v + jnp.sum(dv_low.astype(F32), axis=0, keepdims=True)
    db_ref[:, :width] = db_q
    db_ref[:, width : 2 * width] = db_k
    db_ref[:, 2 * width :] = db_v


def attention_fused(attn_in, w_qkv, b_qkv, grad, w_dense_t, tables):
    width = w_dense_t.shape[1]
    features = attn_in.shape[1]
    return pl.pallas_call(
        functools.partial(attention_kernel, width),
        out_shape=(
            jax.ShapeDtypeStruct((LEN, width), BF16),
            jax.ShapeDtypeStruct((LEN, 3 * width), BF16),
            jax.ShapeDtypeStruct((1, 3 * width), F32),
        ),
        in_specs=[pl.BlockSpec(memory_space=pltpu.VMEM)] * 8,
        out_specs=tuple([pl.BlockSpec(memory_space=pltpu.VMEM)] * 3),
        scratch_shapes=[
            pltpu.VMEM((LEN, width), BF16),
            pltpu.VMEM((LEN, width), BF16),
            pltpu.VMEM((LEN, width), BF16),
            pltpu.VMEM((LEN, width), BF16),
            pltpu.VMEM((width, LEN), BF16),
            pltpu.VMEM((width, LEN), BF16),
            pltpu.VMEM((LEN, width), F32),
            pltpu.VMEM((LEN, width), F32),
        ],
        compiler_params=pltpu.CompilerParams(vmem_limit_bytes=48 * 1024 * 1024),
        cost_estimate=pl.CostEstimate(
            flops=2 * LEN * features * 4 * width + 20 * LEN * LEN * width,
            bytes_accessed=4 * LEN * features + 20 * LEN * width,
            transcendentals=LEN * LEN * width // HD,
        ),
    )(attn_in, w_qkv, b_qkv.reshape(1, -1), grad, w_dense_t, *tables)


def attention_plain(attn_in, w_qkv, b_qkv, grad, w_dense_t, tables):
    width = w_dense_t.shape[1]
    heads = width // HD
    keep, up, down = tables
    half = ROT // 2

    def turn(value, sign):
        return value * keep + sign * (
            jnp.roll(value, -half, 1) * up + jnp.roll(value, half, 1) * down
        )

    def split(value):
        return value.reshape(LEN, heads, HD)

    def product(pattern, left, right):
        return jnp.einsum(pattern, left, right, preferred_element_type=F32)

    proj = mm(attn_in, w_qkv) + b_qkv
    query = split(turn(proj[:, :width], 1.0).astype(BF16))
    key = split(turn(proj[:, width : 2 * width], 1.0).astype(BF16))
    value = split(proj[:, 2 * width :].astype(BF16))
    grad_low = split(mm(grad, w_dense_t).astype(BF16))
    places = jnp.arange(LEN)
    scores = product("qhe,khe->hqk", query, key) * HD ** (-0.5)
    weights = jax.nn.softmax(jnp.where(places[:, None] >= places[None, :], scores, -1e30), axis=-1)
    low = weights.astype(BF16)
    mixed = product("hqk,khe->qhe", low, value).reshape(LEN, width).astype(BF16)
    dweights = product("qhe,khe->hqk", grad_low, value)
    inner = jnp.sum(weights * dweights, axis=-1, keepdims=True)
    dscores = (weights * (dweights - inner)).astype(BF16)
    dq = product("hqk,khe->qhe", dscores, key).reshape(LEN, width) * HD ** (-0.5)
    dk = product("hqk,qhe->khe", dscores, query).reshape(LEN, width) * HD ** (-0.5)
    dv = product("hqk,qhe->khe", low, grad_low).reshape(LEN, width)
    dqkv = jnp.concatenate([turn(dq, -1.0), turn(dk, -1.0), dv], axis=1).astype(BF16)
    return mixed, dqkv, jnp.sum(dqkv.astype(F32), axis=0, keepdims=True)


def normalize(hidden):
    inputs = hidden.astype(F32)
    mean = jnp.mean(inputs, axis=1, keepdims=True)
    square = jnp.mean(inputs * inputs, axis=1, keepdims=True)
    inv_std = lax.rsqrt(square - mean * mean + EPS)
    return (inputs - mean) * inv_std, inv_std


def feed_forward(mlp_in, w_up, b_up, grad, w_down_t):
    pre = mm(mlp_in, w_up) + b_up
    grad_act = mm(grad, w_down_t)
    phi = 0.5 * (1.0 + lax.erf(pre * (0.5 ** 0.5)))
    slope = phi + pre * (jnp.exp(-0.5 * pre * pre) * 0.3989422804014327)
    act = (pre * phi).astype(BF16)
    dpre = (slope * grad_act).astype(BF16)
    return act, dpre, jnp.sum(dpre.astype(F32), axis=0, keepdims=True)


def sequence_pass(hidden, grad, gains, chunks, reduce_chunk):
    normed, inv_std = normalize(hidden)
    attn_in = (normed * gains[0] + gains[1]).astype(BF16)
    mlp_in = (normed * gains[2] + gains[3]).astype(BF16)
    width = chunks[0][2].shape[1]
    fused = width % 128 == 0
    tables = rope_tables(width)
    branch = grad_attn = grad_mlp = None
    weight_grads, bias_grads = [], []

    def add(total, term):
        return term if total is None else total + term

    ffn, att = [], []
    for w_qkv, b_qkv, w_dense_t, w_up, b_up, w_down_t in chunks:
        act, dpre, db_up = feed_forward(mlp_in, w_up, b_up, grad, w_down_t)
        branch = add(branch, mm_t(act, w_down_t))
        grad_mlp = add(grad_mlp, mm_t(dpre, w_up))
        ffn.append((t_mm(mlp_in, dpre), t_mm(grad, act), db_up))
    for w_qkv, b_qkv, w_dense_t, w_up, b_up, w_down_t in chunks:
        attention = attention_fused if fused else attention_plain
        mixed, dqkv, db_qkv = attention(attn_in, w_qkv, b_qkv, grad, w_dense_t, tables)
        branch = add(branch, mm_t(mixed, w_dense_t))
        grad_attn = add(grad_attn, mm_t(dqkv, w_qkv))
        att.append((t_mm(attn_in, dqkv), t_mm(grad, mixed), db_qkv))
    ups = reduce_chunk([item[0] for item in ffn])
    downs = reduce_chunk([item[1] for item in ffn])
    qkvs = reduce_chunk([item[0] for item in att])
    denses = reduce_chunk([item[1] for item in att])
    db_up = jnp.concatenate([item[2] for item in ffn], axis=0)
    db_qkv = jnp.concatenate([item[2] for item in att], axis=0)
    sums = jnp.stack(
        [
            jnp.sum(grad_attn * normed, axis=0),
            jnp.sum(grad_attn, axis=0),
            jnp.sum(grad_mlp * normed, axis=0),
            jnp.sum(grad_mlp, axis=0),
            jnp.sum(grad.astype(F32), axis=0),
        ]
    )
    grad_normed = grad_attn * gains[0] + grad_mlp * gains[2]
    row_sums = jnp.stack([jnp.sum(grad_normed, axis=1), jnp.sum(grad_normed * normed, axis=1)], axis=0)
    return normed, inv_std, branch, grad_normed, row_sums, sums, (qkvs, denses, ups, downs), db_qkv, db_up


def by_part(weight, heads):
    rows = weight.shape[0]
    return weight.reshape(rows, heads, 3, HD).transpose(0, 2, 1, 3).reshape(rows, -1)


def by_head(weight, heads):
    rows = weight.shape[0]
    return weight.reshape(rows, 3, heads, HD).transpose(0, 2, 1, 3).reshape(rows, -1)


BLOCK = 256
COST = 8
PARTS = LEN // BLOCK


def part_rows(part):
    return pl.ds(part * BLOCK, BLOCK)


def call(kernel, outs, args, flops, extra=0, scratch=(), after=(), room=16):
    moved = sum(x.size * x.dtype.itemsize for x in args) + sum(x.size * x.dtype.itemsize for x in outs)
    args, held, count = list(args), len(args), len(after)

    def body(*refs):
        kernel(*refs[:held], *refs[held + count :])

    args = args + list(after)
    return pl.pallas_call(
        body,
        out_shape=tuple(outs),
        in_specs=[pl.BlockSpec(memory_space=pltpu.VMEM)] * held + [pl.BlockSpec(memory_space=pl.ANY)] * count,
        out_specs=tuple([pl.BlockSpec(memory_space=pltpu.VMEM)] * len(outs)),
        scratch_shapes=list(scratch),
        compiler_params=pltpu.CompilerParams(vmem_limit_bytes=moved + room * 1024 * 1024),
        cost_estimate=pl.CostEstimate(flops=flops // COST, bytes_accessed=moved // COST, transcendentals=extra // COST),
    )(*args)


def tie(values, deps):
    values, deps = list(values), list(deps)
    anywhere = pl.BlockSpec(memory_space=pl.ANY)
    return pl.pallas_call(
        lambda *refs: None,
        out_shape=tuple(shape(value.shape, value.dtype) for value in values),
        in_specs=[anywhere] * (len(values) + len(deps)),
        out_specs=(anywhere,) * len(values),
        input_output_aliases={at: at for at in range(len(values))},
        cost_estimate=pl.CostEstimate(flops=1, bytes_accessed=1, transcendentals=0),
    )(*values, *deps)


def shape(dims, kind):
    return jax.ShapeDtypeStruct(dims, kind)


def row_stats(values):
    count = values.shape[1]
    mean = jnp.sum(values, axis=1, keepdims=True) * (1.0 / count)
    square = jnp.sum(values * values, axis=1, keepdims=True) * (1.0 / count)
    return mean, lax.rsqrt(square - mean * mean + EPS)


def joined_rows(mine, other, rows):
    return jnp.concatenate([part[rows, :] for pair in zip(mine, other) for part in pair], axis=1)


def grad_kernel(*refs):
    mine, other, (g_ref, gt_ref, sum_ref) = refs[:4], refs[4:8], refs[8:]
    total = jnp.zeros(sum_ref.shape, F32)
    for part in range(PARTS):
        rows = part_rows(part)
        value = joined_rows(mine, other, rows)
        wide = value.astype(F32)
        g_ref[rows, :] = value
        gt_ref[:, rows] = wide.T.astype(BF16)
        total = total + jnp.sum(wide, axis=0, keepdims=True)
    sum_ref[...] = total


def norm_kernel(*refs):
    mine, other, vec_ref, (a_ref, at_ref, m_ref, mt_ref) = refs[:4], refs[4:8], refs[8], refs[9:]
    for part in range(PARTS):
        rows = part_rows(part)
        value = joined_rows(mine, other, rows).astype(F32)
        mean, inv_std = row_stats(value)
        normed = (value - mean) * inv_std
        attn = normed * vec_ref[0:1, :] + vec_ref[1:2, :]
        a_ref[rows, :] = attn.astype(BF16)
        at_ref[:, rows] = attn.T.astype(BF16)
        mlp = normed * vec_ref[2:3, :] + vec_ref[3:4, :]
        m_ref[rows, :] = mlp.astype(BF16)
        mt_ref[:, rows] = mlp.T.astype(BF16)


def attention_box_kernel(width, count, x_ref, xt_ref, g_ref, gt_ref, keep_ref, up_ref, down_ref, *refs):
    packs, biases, refs = refs[:count], refs[count : 2 * count], refs[2 * count :]
    outs, scratch = refs[: 4 * count], refs[4 * count :]
    for at in range(count):
        heads_ref, dqkv_ref, db_ref, dw_ref = outs[4 * at : 4 * at + 4]
        pack_ref = packs[at]
        attention_kernel(
            width, x_ref, pack_ref.at[:, : 3 * width], biases[at], g_ref, pack_ref.at[:, 3 * width :], keep_ref,
            up_ref, down_ref, heads_ref, dqkv_ref, db_ref, *scratch,
        )
        for part in range(PARTS):
            rows = part_rows(part)
            dw_ref[rows, : 3 * width] = mm(xt_ref[rows, :], dqkv_ref[...]).astype(BF16)
            dw_ref[rows, 3 * width :] = mm(gt_ref[rows, :], heads_ref[...]).astype(BF16)


def attention_box(attn_in, attn_t, packs, biases, grad, grad_t, tables, after):
    width = packs[0].shape[1] // 4
    features = attn_in.shape[1]
    count = len(packs)
    square = pltpu.VMEM((LEN, width), BF16)
    turned = pltpu.VMEM((width, LEN), BF16)
    sums = pltpu.VMEM((LEN, width), F32)
    out = [shape((LEN, width), BF16), shape((LEN, 3 * width), BF16), shape((1, 3 * width), F32), shape(packs[0].shape, BF16)]
    outs = call(
        functools.partial(attention_box_kernel, width, count),
        out * count,
        [attn_in, attn_t, grad, grad_t, *tables, *packs, *biases],
        flops=count * (2 * LEN * features * 8 * width + 20 * LEN * LEN * width),
        extra=LEN * LEN * width // HD,
        scratch=[square] * 4 + [turned] * 2 + [sums] * 2,
        after=after,
    )
    return [outs[4 * at : 4 * at + 4] for at in range(count)]


def feed_box_kernel(count, x_ref, xt_ref, g_ref, gt_ref, *refs):
    ups, downs, biases, outs = refs[:count], refs[count : 2 * count], refs[2 * count : 3 * count], refs[3 * count :]
    for at in range(count):
        act_ref, dpre_ref, db_ref, dup_ref, ddown_ref = outs[5 * at : 5 * at + 5]
        total = jnp.zeros(db_ref.shape, F32)
        bias = biases[at][...]
        for part in range(PARTS):
            rows = part_rows(part)
            pre = mm(x_ref[rows, :], ups[at][...]) + bias
            grad_act = mm(g_ref[rows, :], downs[at][...])
            phi = 0.5 + 0.5 * lax.erf(pre * (0.5 ** 0.5))
            slope = phi + pre * (jnp.exp(-0.5 * pre * pre) * 0.3989422804014327)
            act_ref[rows, :] = (pre * phi).astype(BF16)
            dpre = (slope * grad_act).astype(BF16)
            dpre_ref[rows, :] = dpre
            total = total + jnp.sum(dpre.astype(F32), axis=0, keepdims=True)
        db_ref[...] = total
        for part in range(PARTS):
            rows = part_rows(part)
            dup_ref[rows, :] = mm(xt_ref[rows, :], dpre_ref[...]).astype(BF16)
            ddown_ref[rows, :] = mm(gt_ref[rows, :], act_ref[...]).astype(BF16)


def feed_box(mlp_in, mlp_t, ups, downs, biases, grad, grad_t, after):
    columns = ups[0].shape[1]
    features = mlp_in.shape[1]
    count = len(ups)
    out = [shape((LEN, columns), BF16)] * 2 + [shape((1, columns), F32)] + [shape(ups[0].shape, BF16)] * 2
    outs = call(
        functools.partial(feed_box_kernel, count),
        out * count,
        [mlp_in, mlp_t, grad, grad_t, *ups, *downs, *biases],
        flops=count * 8 * LEN * features * columns,
        extra=2 * LEN * columns,
        after=after,
    )
    return [outs[5 * at : 5 * at + 5] for at in range(count)]


def out_kernel(half, *refs):
    heads, acts, apacks, downs, (keep_ref, send_ref) = refs[:4], refs[4:8], refs[8:12], refs[12:16], refs[16:]
    width = heads[0].shape[1]
    for part in range(PARTS):
        rows = part_rows(part)
        total = None
        for k in range(4):
            term = mm_t(acts[k][rows, :], downs[k][...]) + mm_t(heads[k][rows, :], apacks[k][:, 3 * width :])
            total = term if total is None else total + term
        for k in range(4):
            to = slice(k * half, (k + 1) * half)
            keep_ref[rows, to] = total[:, 2 * k * half : (2 * k + 1) * half]
            send_ref[rows, to] = total[:, (2 * k + 1) * half : (2 * k + 2) * half].astype(BF16)


def in_kernel(half, *refs):
    mine, other, vec_ref = refs[:4], refs[4:8], refs[8]
    dqkvs, dpres, apacks, ups = refs[9:13], refs[13:17], refs[17:21], refs[21:25]
    keep_ref, send_ref, row_ref, sum_ref = refs[25:]
    width3 = dqkvs[0].shape[1]
    lane = lax.broadcasted_iota(jnp.int32, (BLOCK, 128), 1)
    sums = [jnp.zeros((1, sum_ref.shape[1]), F32) for _ in range(4)]
    for part in range(PARTS):
        rows = part_rows(part)
        grad_attn = grad_mlp = None
        for k in range(4):
            first = mm_t(dqkvs[k][rows, :], apacks[k][:, :width3])
            second = mm_t(dpres[k][rows, :], ups[k][...])
            grad_attn = first if k == 0 else grad_attn + first
            grad_mlp = second if k == 0 else grad_mlp + second
        value = joined_rows(mine, other, rows).astype(F32)
        mean, inv_std = row_stats(value)
        normed = (value - mean) * inv_std
        for at, term in enumerate((grad_attn * normed, grad_attn, grad_mlp * normed, grad_mlp)):
            sums[at] = sums[at] + jnp.sum(term, axis=0, keepdims=True)
        total = grad_attn * vec_ref[0:1, :] + grad_mlp * vec_ref[2:3, :]
        plain = jnp.sum(total, axis=1, keepdims=True)
        cross = jnp.sum(total * normed, axis=1, keepdims=True)
        both = jnp.where(lane == 0, plain, jnp.where(lane == 1, cross, 0.0))
        row_ref[:, rows] = both.T[:8, :]
        for k in range(4):
            to = slice(k * half, (k + 1) * half)
            keep_ref[rows, to] = total[:, 2 * k * half : (2 * k + 1) * half]
            send_ref[rows, to] = total[:, (2 * k + 1) * half : (2 * k + 2) * half].astype(BF16)
    for at in range(4):
        sum_ref[at : at + 1, :] = sums[at]


def final_kernel(features, half, *refs):
    mine, other, grads = refs[:4], refs[4:8], refs[8:12]
    keep_ref, got_ref, row_ref = refs[12:15]
    outs = refs[15:]
    for part in range(PARTS):
        rows = part_rows(part)
        mean, inv_std = row_stats(joined_rows(mine, other, rows).astype(F32))
        padded = jnp.concatenate([row_ref[:, rows], jnp.zeros((120, BLOCK), F32)], axis=0).T
        plain = padded[:, 0:1] * (1.0 / features)
        cross = padded[:, 1:2] * (1.0 / features)
        for k in range(4):
            to = slice(k * half, (k + 1) * half)
            total = keep_ref[rows, to] + got_ref[rows, to].astype(F32)
            normed = (mine[k][rows, :].astype(F32) - mean) * inv_std
            outs[k][rows, :] = (grads[k][rows, :].astype(F32) + inv_std * (total - plain - normed * cross)).astype(BF16)


def weights_kernel(heads, place_ref, *refs):
    att, ups, downs, (qkv_ref, dense_ref, up_ref, down_ref) = refs[:4], refs[4:8], refs[8:12], refs[12:]
    dp, gx = place_ref[0], place_ref[1]
    width, columns = att[0].shape[1] // 4, ups[0].shape[1]
    half = att[0].shape[0] // 2
    for k in range(4):
        quarter = dp ^ k
        for part in range(2):
            rows = pl.ds(part * half, half)
            to = pl.ds(pl.multiple_of((gx ^ part) * half, half), half)
            value = att[k][rows, :].astype(F32)
            pieces = [
                value[:, kind * width + head * HD : kind * width + (head + 1) * HD]
                for head in range(heads) for kind in range(3)
            ]
            qkv_ref[to, pl.ds(pl.multiple_of(quarter * 3 * width, 128), 3 * width)] = jnp.concatenate(pieces, axis=1)
            dense_ref[pl.ds(pl.multiple_of(quarter * width, 128), width), to] = value[:, 3 * width :].T
            up_ref[to, pl.ds(pl.multiple_of(quarter * columns, 128), columns)] = ups[k][rows, :].astype(F32)
            down_ref[pl.ds(pl.multiple_of(quarter * columns, 128), columns), to] = downs[k][rows, :].astype(F32).T


def local_box(
    hidden_in, ln1_gain, ln1_bias, ln2_gain, ln2_bias, w_qkv, b_qkv, w_dense, b_dense, w_up, b_up,
    w_down, b_down, cotangent,
):
    dp, gx, gy = lax.axis_index("dp"), lax.axis_index("gx"), lax.axis_index("gy")
    wide = hidden_in.shape[1]
    features = 4 * wide
    half = wide // 2
    lower = gx == 0
    aligned = (gy // 2) == gx
    odd = (gy % 2) == 1

    def rel_rows(value):
        return jnp.where(lower, value, jnp.roll(value, -half, axis=0))

    def cut_half(value):
        value = value.reshape(2, LEN, wide)
        first, second = value[:, :, :half], value[:, :, half:]
        return jnp.where(lower, first, second), jnp.where(lower, second, first)

    def pieces_of(kept, got):
        near = jnp.where(aligned, kept, got)
        far = jnp.where(aligned, got, kept)
        return [
            jnp.where(odd, near[1], near[0]), jnp.where(odd, near[0], near[1]),
            jnp.where(odd, far[1], far[0]), jnp.where(odd, far[0], far[1]),
        ]

    def exchange_z(pieces, deps):
        if deps:
            pieces = [pieces[0]] + list(tie(pieces[1:], deps))
        return [pieces[0]] + [swap(pieces[k], "gy", k, 4) for k in (1, 2, 3)]

    def from_half(got):
        near = jnp.stack([jnp.where(odd, got[1], got[0]), jnp.where(odd, got[0], got[1])])
        far = jnp.stack([jnp.where(odd, got[3], got[2]), jnp.where(odd, got[2], got[3])])
        own = jnp.where(aligned, near, far)
        back = swap(jnp.where(aligned, far, near), "gx", 1, 2)
        first = jnp.where(lower, own, back)
        second = jnp.where(lower, back, own)
        return jnp.concatenate([first, second], axis=2).reshape(2 * LEN, wide)

    heads = w_qkv.shape[1] // (3 * HD) // 4

    def columns_of(value):
        return lax.dynamic_slice_in_dim(value, dp * (value.shape[1] // 4), value.shape[1] // 4, 1)

    def rows_of(value):
        return lax.dynamic_slice_in_dim(value, dp * (value.shape[0] // 4), value.shape[0] // 4, 0).T

    def gather_z(value, deps=()):
        sent = tie([value], deps)[0] if deps else value
        return [sent] + [swap(sent, "gy", k, 4) for k in (1, 2, 3)]

    def spread(value):
        block = jnp.concatenate(value, axis=0)
        core = swap(block, "dp", 1, 4)
        across = swap(block, "dp", 2, 4)
        return [block, core, across, swap(across, "dp", 1, 4)]

    att_z = gather_z(rel_rows(jnp.concatenate([by_part(columns_of(w_qkv), heads), rows_of(w_dense)], axis=1)))
    vectors = rel_rows(jnp.stack([ln1_gain, ln1_bias, ln2_gain, ln2_bias, b_dense + b_down]).T).T
    vectors = jnp.concatenate(gather_z(vectors), axis=1)
    up_own, down_own = rel_rows(columns_of(w_up)), rel_rows(rows_of(w_down))
    hidden_kept, hidden_sent = cut_half(hidden_in)
    hidden_got = swap(hidden_sent, "gx", 1, 2)
    grad_kept, grad_sent = cut_half(cotangent)
    grad_got = swap(tie([grad_sent], [hidden_got])[0], "gx", 1, 2)
    hidden_half = exchange_z(pieces_of(hidden_kept, hidden_got), att_z[1:])
    hidden_other = [swap(piece, "gx", 1, 2) for piece in hidden_half]
    att_packs = spread(att_z)
    grad_half = exchange_z(pieces_of(grad_kept, grad_got), hidden_half[1:] + [att_packs[1]])
    grad_other = [swap(piece, "gx", 1, 2) for piece in grad_half]

    square = shape((LEN, features), BF16)
    attn_in, attn_t, mlp_in, mlp_t = call(
        norm_kernel, [square] * 4, [*hidden_half, *hidden_other, vectors], flops=20 * LEN * features
    )
    up_z = gather_z(up_own, grad_half[1:] + hidden_other[1:] + att_packs[2:3])
    ups = spread(up_z)
    down_z = gather_z(down_own, up_z[1:] + [attn_in])
    downs = spread(down_z)
    b_qkv_c = xor_order(by_part(b_qkv.reshape(4, -1), heads), dp, 4)
    b_up_c = xor_order(b_up.reshape(4, -1), dp, 4)

    grad, grad_t, grad_sum = call(
        grad_kernel, [square, square, shape((1, features), F32)], [*grad_half, *grad_other], flops=4 * LEN * features,
        after=[attn_in] + up_z[1:],
    )
    tables = rope_tables(att_packs[0].shape[1] // 4)

    mixed, dqkv, db_qkv, acts, dpre, db_up, att_sums, up_sums, down_sums = [[None] * 4 for _ in range(9)]

    def attention(pair, after):
        outs = attention_box(
            attn_in, attn_t, [att_packs[k] for k in pair], [b_qkv_c[k : k + 1] for k in pair], grad, grad_t, tables, after
        )
        for k, out in zip(pair, outs):
            mixed[k], dqkv[k], db_qkv[k], att_sums[k] = out

    def feed(pair, after):
        outs = feed_box(
            mlp_in, mlp_t, [ups[k] for k in pair], [downs[k] for k in pair], [b_up_c[k : k + 1] for k in pair], grad,
            grad_t, after,
        )
        for k, out in zip(pair, outs):
            acts[k], dpre[k], db_up[k], up_sums[k], down_sums[k] = out

    def far_sum(sums):
        return (sums[2].astype(F32) + swap(sums[3], "dp", 1, 4).astype(F32)).astype(BF16)

    def whole_sum(sums, far):
        total = sums[0].astype(F32) + swap(sums[1], "dp", 1, 4).astype(F32) + far.astype(F32)
        blocks = total.reshape(4, wide, -1)
        low = blocks[1:].astype(BF16)
        return blocks[0], [low[0], low[1], low[2]]

    def sum_z(blocks, deps):
        got = exchange_z([None] + blocks[1], deps)
        return blocks[0], got[1:]

    def quarters(own, got):
        mine = (own + got[0].astype(F32) + got[1].astype(F32) + got[2].astype(F32)).astype(BF16)
        across = swap(mine, "dp", 2, 4)
        return [mine, swap(mine, "dp", 1, 4), across, swap(across, "dp", 1, 4)]

    attention((3, 2), [])
    attention((1, 0), down_z[1:] + [ups[2], mixed[2]])
    att_far = far_sum(att_sums)
    feed((3, 2), [att_far, mixed[0]])
    att_far = swap(att_far, "dp", 2, 4)
    feed((1, 0), [acts[2]])
    up_far, down_far = far_sum(up_sums), far_sum(down_sums)
    att_own, att_got = sum_z(whole_sum(att_sums, att_far), [])
    up_far_got = swap(up_far, "dp", 2, 4)
    down_far_got = swap(tie([down_far], [up_far_got])[0], "dp", 2, 4)

    out_flops = 2 * LEN * features * (4 * acts[0].shape[1] + 4 * mixed[0].shape[1])
    keep, send = call(
        functools.partial(out_kernel, half),
        [shape((LEN, 4 * half), F32), shape((LEN, 4 * half), BF16)],
        [*mixed, *acts, *att_packs, *downs],
        flops=out_flops,
        after=[att_far, up_far, down_far],
    )
    out_send = send
    got = swap(send, "gx", 1, 2)
    out_half = [
        (
            hidden_half[k].astype(F32)
            + keep[:, k * half : (k + 1) * half]
            + got[:, k * half : (k + 1) * half].astype(F32)
            + vectors[4:5, 2 * k * half : (2 * k + 1) * half]
        ).astype(BF16)
        for k in range(4)
    ]
    up_own, up_got = sum_z(whole_sum(up_sums, up_far_got), att_got)
    out_z = exchange_z(out_half, up_got)
    hidden_out = from_half(out_z)
    down_own, down_got = sum_z(whole_sum(down_sums, down_far_got), out_z[1:])

    keep, send, row_sums, sums = call(
        functools.partial(in_kernel, half),
        [shape((LEN, 4 * half), F32), shape((LEN, 4 * half), BF16), shape((8, LEN), F32), shape((4, features), F32)],
        [*hidden_half, *hidden_other, vectors, *dqkv, *dpre, *att_packs, *ups],
        flops=2 * LEN * features * (4 * dpre[0].shape[1] + 4 * dqkv[0].shape[1]),
        after=[out_send, up_far_got] + att_got,
    )
    got = swap(send, "gx", 1, 2)
    row_sums = row_sums + swap(row_sums, "gx", 1, 2)
    in_half = call(
        functools.partial(final_kernel, features, half),
        [shape((LEN, half), BF16)] * 4,
        [*hidden_half, *hidden_other, *grad_half, keep, got, row_sums],
        flops=10 * LEN * features,
    )
    grad_input = from_half(exchange_z(list(in_half), down_got))
    att_grads, up_grads = quarters(att_own, att_got), quarters(up_own, up_got)
    down_grads = quarters(down_own, down_got)

    sums = jnp.concatenate([sums, 0.5 * grad_sum], axis=0).reshape(5, 4, 2, half)
    sums = xor_order(xor_order(sums.transpose(1, 0, 2, 3), gy, 4).transpose(2, 0, 1, 3), gx, 2)
    db_qkv = by_head(jnp.concatenate(db_qkv, axis=0), heads)
    db = xor_order(jnp.concatenate([db_qkv, jnp.concatenate(db_up, axis=0)], axis=1), dp, 4).reshape(1, -1)
    db = jnp.concatenate([db, jnp.zeros_like(db)], axis=0)
    db = jnp.where(lower, db, db[::-1])
    both = jnp.concatenate([sums.reshape(-1, 128), db.reshape(-1, 128)], axis=0)
    for axis, step, count in (("dp", 1, 4), ("dp", 2, 4), ("gx", 1, 2), ("gy", 1, 4), ("gy", 2, 4)):
        both = both + swap(both, axis, step, count)
    split = sums.size // 128
    sums = both[:split].reshape(2, 4, 5, half)
    mine = lax.dynamic_index_in_dim(sums, gy, 1, keepdims=False).transpose(1, 0, 2).reshape(5, wide)
    db = lax.dynamic_index_in_dim(both[split:].reshape(2, 4, -1), gx, 0, keepdims=False)
    columns = db_qkv.shape[1]

    place = jnp.stack([dp, gx]).astype(jnp.int32)
    vmem = pl.BlockSpec(memory_space=pltpu.VMEM)
    grad_w_qkv, grad_w_dense, grad_w_up, grad_w_down = pl.pallas_call(
        functools.partial(weights_kernel, heads),
        out_shape=tuple(shape(value.shape, F32) for value in (w_qkv, w_dense, w_up, w_down)),
        in_specs=[pl.BlockSpec(memory_space=pltpu.SMEM)] + [vmem] * 12,
        out_specs=(vmem,) * 4,
        compiler_params=pltpu.CompilerParams(vmem_limit_bytes=24 * 1024 * 1024),
    )(place, *att_grads, *up_grads, *down_grads)
    return (
        hidden_out, grad_input, mine[0], mine[1], mine[2], mine[3], grad_w_qkv, db[:, :columns].reshape(-1),
        grad_w_dense, mine[4], grad_w_up, db[:, columns:].reshape(-1), grad_w_down, mine[4],
    )


def local_any(
    gx_count, gy_count,
    hidden_in, ln1_gain, ln1_bias, ln2_gain, ln2_bias, w_qkv, b_qkv, w_dense, b_dense, w_up, b_up,
    w_down, b_down, cotangent,
):
    heads = w_qkv.shape[1] // (3 * HD)

    def to_sequence(value):
        rows = lax.all_gather(value, "gx", axis=0, tiled=True)
        return lax.all_to_all(rows, "gy", split_axis=0, concat_axis=1, tiled=True)

    def from_sequence(value):
        return lax.all_to_all(value, "gy", split_axis=1, concat_axis=0, tiled=True)

    def gather(value):
        return lax.all_gather(value, "gy", axis=0, tiled=True)

    hidden, grad = to_sequence(hidden_in), to_sequence(cotangent)
    vectors = jnp.stack([ln1_gain, ln1_bias, ln2_gain, ln2_bias])
    vectors = lax.all_gather(vectors, "gy", axis=1, tiled=True)
    chunk = (
        gather(by_part(w_qkv, heads)),
        by_part(b_qkv[None], heads)[0],
        gather(w_dense.T),
        gather(w_up),
        b_up,
        gather(w_down.T),
    )

    def reduce_chunk(grads):
        return lax.psum(lax.psum_scatter(grads[0], "gy", scatter_dimension=0, tiled=True), "dp")

    normed, inv_std, branch, grad_normed, row_sums, sums, reduced, db_qkv, db_up = sequence_pass(
        hidden, grad, vectors, [chunk], reduce_chunk
    )
    branch_rows = lax.psum_scatter(from_sequence(branch), "gx", scatter_dimension=0, tiled=True)
    hidden_out = (hidden_in.astype(F32) + branch_rows + b_dense + b_down).astype(BF16)
    features = normed.shape[1]
    row_sums = lax.psum(row_sums, "gx")
    grad_normed = grad_normed - (
        row_sums[0][:, None] / features + normed * (row_sums[1][:, None] / features)
    ) * (1.0 / gx_count)
    grad_rows = lax.psum_scatter(from_sequence(inv_std * grad_normed), "gx", scatter_dimension=0, tiled=True)
    grad_input = (cotangent.astype(F32) + grad_rows).astype(BF16)
    sums = lax.psum_scatter(sums, "gy", scatter_dimension=1, tiled=True)
    sums = lax.psum(sums * jnp.array([1.0] * 4 + [1.0 / gx_count], F32)[:, None], ("dp", "gx"))
    db_qkv, db_up = lax.psum((by_head(db_qkv, heads)[0], db_up[0]), ("dp", "gy"))
    qkvs, denses, ups, downs = reduced
    return (
        hidden_out, grad_input, sums[0], sums[1], sums[2], sums[3], by_head(qkvs, heads), db_qkv,
        denses.T, sums[4], ups, db_up, downs.T, sums[4],
    )


def solution(mesh):
    sizes = mesh.shape
    boxed = sizes["dp"] == 4 and sizes["gx"] == 2 and sizes["gy"] == 4
    rows, feature = P(("dp", "gx"), "gy"), P("gy")
    placed = (
        rows, feature, feature, feature, feature, P("gy", "gx"), P("gx"), P("gx", "gy"), feature,
        P("gy", "gx"), P("gx"), P("gx", "gy"), feature, rows,
    )
    return jax.shard_map(
        local_box if boxed else functools.partial(local_any, sizes["gx"], sizes["gy"]),
        mesh=mesh,
        in_specs=placed,
        out_specs=(rows, rows) + placed[1:5] + placed[5:13],
        check_vma=False,
    )
```

```python
import functools

import jax
import jax.numpy as jnp
from jax import lax
from jax.experimental import pallas as pl
from jax.experimental.pallas import tpu as pltpu
from jax.sharding import PartitionSpec as P

HD = 64
ROT = 16
LEN = 1024
EPS = 1e-05
F32 = jnp.float32
BF16 = jnp.bfloat16


def mm(left, right):
    return jnp.dot(left, right, preferred_element_type=F32)


def mm_t(left, right):
    return lax.dot_general(left, right, (((1,), (1,)), ((), ())), preferred_element_type=F32)


def t_mm(left, right):
    return lax.dot_general(left, right, (((0,), (0,)), ((), ())), preferred_element_type=F32)


def swap(value, axis, step, count):
    return lax.ppermute(value, axis, [(i, i ^ step) for i in range(count)])


def xor_order(value, index, count):
    rest = value.shape[1:]
    bit = 1
    while bit < count:
        paired = value.reshape((count // (2 * bit), 2, bit) + rest)
        turned = paired[:, ::-1]
        value = jnp.where((index & bit) != 0, turned, paired).reshape((count,) + rest)
        bit *= 2
    return value


def rope_tables(width):
    place = lax.broadcasted_iota(jnp.int32, (LEN, width), 0).astype(F32)
    lane = lax.broadcasted_iota(jnp.int32, (LEN, width), 1) % HD
    half = ROT // 2
    turned = place * 10000.0 ** (-(lane % half).astype(F32) * 2.0 / ROT)
    cosine, sine = jnp.cos(turned), jnp.sin(turned)
    keep = jnp.where(lane < ROT, cosine, 1.0)
    from_up = jnp.where(lane < half, -sine, 0.0)
    from_down = jnp.where((lane >= half) & (lane < ROT), sine, 0.0)
    return keep, from_up, from_down


def attention_kernel(
    width, x_ref, wq_ref, b_ref, g_ref, wd_ref, keep_ref, up_ref, down_ref,
    heads_ref, dqkv_ref, db_ref, q_s, k_s, v_s, g_s, kt_s, vt_s, dk_s, dv_s,
):
    heads = width // HD
    half = ROT // 2
    block = 256
    scale = HD ** (-0.5)
    b_row = b_ref[...]

    def turn(value, rows, sign):
        return (
            value * keep_ref[rows, :]
            + sign * (pltpu.roll(value, width - half, 1) * up_ref[rows, :])
            + sign * (pltpu.roll(value, half, 1) * down_ref[rows, :])
        )

    for part in range(LEN // block):
        rows = pl.ds(part * block, block)
        proj = mm(x_ref[rows, :], wq_ref[...]) + b_row
        q_s[rows, :] = turn(proj[:, :width], rows, 1.0).astype(BF16)
        key = turn(proj[:, width : 2 * width], rows, 1.0)
        value = proj[:, 2 * width :]
        k_s[rows, :] = key.astype(BF16)
        v_s[rows, :] = value.astype(BF16)
        kt_s[:, rows] = key.T.astype(BF16)
        vt_s[:, rows] = value.T.astype(BF16)
        g_s[rows, :] = mm(g_ref[rows, :], wd_ref[...]).astype(BF16)

    dk_s[...] = jnp.zeros_like(dk_s)
    dv_s[...] = jnp.zeros_like(dv_s)
    lane_head = lax.broadcasted_iota(jnp.int32, (block, width), 1) // HD
    key_at = lax.broadcasted_iota(jnp.int32, (block, block), 0)
    query_at = lax.broadcasted_iota(jnp.int32, (block, block), 1)
    seen = key_at <= query_at
    db_q = jnp.zeros((1, width), F32)
    for part in range(LEN // block):
        rows = pl.ds(part * block, block)
        span = (part + 1) * block
        q_block, g_block = q_s[rows, :], g_s[rows, :]
        outs, dqs = [], []
        dk_new, dv_new = None, None
        for head in range(heads):
            own = lane_head == head
            q_own = jnp.where(own, q_block, jnp.zeros_like(q_block))
            g_own = jnp.where(own, g_block, jnp.zeros_like(g_block))
            scores = mm_t(k_s[:span, :], q_own)
            last = jnp.where(seen, scores[span - block :, :], -1e30)
            scores = last if part == 0 else jnp.concatenate([scores[: span - block, :], last], axis=0)
            top = jnp.max(scores, axis=0, keepdims=True)
            exponent = jnp.exp((scores - top) * scale)
            weights = exponent * (1.0 / jnp.sum(exponent, axis=0, keepdims=True))
            low = weights.astype(BF16)
            dweights = mm_t(v_s[:span, :], g_own)
            inner = jnp.sum(weights * dweights, axis=0, keepdims=True)
            dscores = (weights * (dweights - inner)).astype(BF16)
            at = slice(head * HD, (head + 1) * HD)
            outs.append(mm(vt_s[at, :span], low))
            dqs.append(mm(kt_s[at, :span], dscores))
            dv_here, dk_here = mm(low, g_own), mm(dscores, q_own)
            dv_new = dv_here if dv_new is None else dv_new + dv_here
            dk_new = dk_here if dk_new is None else dk_new + dk_here
        dk_s[:span, :] += dk_new
        dv_s[:span, :] += dv_new
        heads_ref[rows, :] = jnp.concatenate(outs, axis=0).T.astype(BF16)
        dq = jnp.concatenate(dqs, axis=0).T * scale
        dq_low = turn(dq, rows, -1.0).astype(BF16)
        dqkv_ref[rows, :width] = dq_low
        db_q = db_q + jnp.sum(dq_low.astype(F32), axis=0, keepdims=True)
    db_k = jnp.zeros((1, width), F32)
    db_v = jnp.zeros((1, width), F32)
    for part in range(LEN // block):
        rows = pl.ds(part * block, block)
        dk_low = turn(dk_s[rows, :] * scale, rows, -1.0).astype(BF16)
        dv_low = dv_s[rows, :].astype(BF16)
        dqkv_ref[rows, width : 2 * width] = dk_low
        dqkv_ref[rows, 2 * width :] = dv_low
        db_k = db_k + jnp.sum(dk_low.astype(F32), axis=0, keepdims=True)
        db_v = db_v + jnp.sum(dv_low.astype(F32), axis=0, keepdims=True)
    db_ref[:, :width] = db_q
    db_ref[:, width : 2 * width] = db_k
    db_ref[:, 2 * width :] = db_v


def attention_fused(attn_in, w_qkv, b_qkv, grad, w_dense_t, tables):
    width = w_dense_t.shape[1]
    features = attn_in.shape[1]
    return pl.pallas_call(
        functools.partial(attention_kernel, width),
        out_shape=(
            jax.ShapeDtypeStruct((LEN, width), BF16),
            jax.ShapeDtypeStruct((LEN, 3 * width), BF16),
            jax.ShapeDtypeStruct((1, 3 * width), F32),
        ),
        in_specs=[pl.BlockSpec(memory_space=pltpu.VMEM)] * 8,
        out_specs=tuple([pl.BlockSpec(memory_space=pltpu.VMEM)] * 3),
        scratch_shapes=[
            pltpu.VMEM((LEN, width), BF16),
            pltpu.VMEM((LEN, width), BF16),
            pltpu.VMEM((LEN, width), BF16),
            pltpu.VMEM((LEN, width), BF16),
            pltpu.VMEM((width, LEN), BF16),
            pltpu.VMEM((width, LEN), BF16),
            pltpu.VMEM((LEN, width), F32),
            pltpu.VMEM((LEN, width), F32),
        ],
        compiler_params=pltpu.CompilerParams(vmem_limit_bytes=48 * 1024 * 1024),
        cost_estimate=pl.CostEstimate(
            flops=2 * LEN * features * 4 * width + 20 * LEN * LEN * width,
            bytes_accessed=4 * LEN * features + 20 * LEN * width,
            transcendentals=LEN * LEN * width // HD,
        ),
    )(attn_in, w_qkv, b_qkv.reshape(1, -1), grad, w_dense_t, *tables)


def attention_plain(attn_in, w_qkv, b_qkv, grad, w_dense_t, tables):
    width = w_dense_t.shape[1]
    heads = width // HD
    keep, up, down = tables
    half = ROT // 2

    def turn(value, sign):
        return value * keep + sign * (
            jnp.roll(value, -half, 1) * up + jnp.roll(value, half, 1) * down
        )

    def split(value):
        return value.reshape(LEN, heads, HD)

    def product(pattern, left, right):
        return jnp.einsum(pattern, left, right, preferred_element_type=F32)

    proj = mm(attn_in, w_qkv) + b_qkv
    query = split(turn(proj[:, :width], 1.0).astype(BF16))
    key = split(turn(proj[:, width : 2 * width], 1.0).astype(BF16))
    value = split(proj[:, 2 * width :].astype(BF16))
    grad_low = split(mm(grad, w_dense_t).astype(BF16))
    places = jnp.arange(LEN)
    scores = product("qhe,khe->hqk", query, key) * HD ** (-0.5)
    weights = jax.nn.softmax(jnp.where(places[:, None] >= places[None, :], scores, -1e30), axis=-1)
    low = weights.astype(BF16)
    mixed = product("hqk,khe->qhe", low, value).reshape(LEN, width).astype(BF16)
    dweights = product("qhe,khe->hqk", grad_low, value)
    inner = jnp.sum(weights * dweights, axis=-1, keepdims=True)
    dscores = (weights * (dweights - inner)).astype(BF16)
    dq = product("hqk,khe->qhe", dscores, key).reshape(LEN, width) * HD ** (-0.5)
    dk = product("hqk,qhe->khe", dscores, query).reshape(LEN, width) * HD ** (-0.5)
    dv = product("hqk,qhe->khe", low, grad_low).reshape(LEN, width)
    dqkv = jnp.concatenate([turn(dq, -1.0), turn(dk, -1.0), dv], axis=1).astype(BF16)
    return mixed, dqkv, jnp.sum(dqkv.astype(F32), axis=0, keepdims=True)


def normalize(hidden):
    inputs = hidden.astype(F32)
    mean = jnp.mean(inputs, axis=1, keepdims=True)
    square = jnp.mean(inputs * inputs, axis=1, keepdims=True)
    inv_std = lax.rsqrt(square - mean * mean + EPS)
    return (inputs - mean) * inv_std, inv_std


def feed_forward(mlp_in, w_up, b_up, grad, w_down_t):
    pre = mm(mlp_in, w_up) + b_up
    grad_act = mm(grad, w_down_t)
    phi = 0.5 * (1.0 + lax.erf(pre * (0.5 ** 0.5)))
    slope = phi + pre * (jnp.exp(-0.5 * pre * pre) * 0.3989422804014327)
    act = (pre * phi).astype(BF16)
    dpre = (slope * grad_act).astype(BF16)
    return act, dpre, jnp.sum(dpre.astype(F32), axis=0, keepdims=True)


def sequence_pass(hidden, grad, gains, chunks, reduce_chunk):
    normed, inv_std = normalize(hidden)
    attn_in = (normed * gains[0] + gains[1]).astype(BF16)
    mlp_in = (normed * gains[2] + gains[3]).astype(BF16)
    width = chunks[0][2].shape[1]
    fused = width % 128 == 0
    tables = rope_tables(width)
    branch = grad_attn = grad_mlp = None
    weight_grads, bias_grads = [], []

    def add(total, term):
        return term if total is None else total + term

    ffn, att = [], []
    for w_qkv, b_qkv, w_dense_t, w_up, b_up, w_down_t in chunks:
        act, dpre, db_up = feed_forward(mlp_in, w_up, b_up, grad, w_down_t)
        branch = add(branch, mm_t(act, w_down_t))
        grad_mlp = add(grad_mlp, mm_t(dpre, w_up))
        ffn.append((t_mm(mlp_in, dpre), t_mm(grad, act), db_up))
    for w_qkv, b_qkv, w_dense_t, w_up, b_up, w_down_t in chunks:
        attention = attention_fused if fused else attention_plain
        mixed, dqkv, db_qkv = attention(attn_in, w_qkv, b_qkv, grad, w_dense_t, tables)
        branch = add(branch, mm_t(mixed, w_dense_t))
        grad_attn = add(grad_attn, mm_t(dqkv, w_qkv))
        att.append((t_mm(attn_in, dqkv), t_mm(grad, mixed), db_qkv))
    ups = reduce_chunk([item[0] for item in ffn])
    downs = reduce_chunk([item[1] for item in ffn])
    qkvs = reduce_chunk([item[0] for item in att])
    denses = reduce_chunk([item[1] for item in att])
    db_up = jnp.concatenate([item[2] for item in ffn], axis=0)
    db_qkv = jnp.concatenate([item[2] for item in att], axis=0)
    sums = jnp.stack(
        [
            jnp.sum(grad_attn * normed, axis=0),
            jnp.sum(grad_attn, axis=0),
            jnp.sum(grad_mlp * normed, axis=0),
            jnp.sum(grad_mlp, axis=0),
            jnp.sum(grad.astype(F32), axis=0),
        ]
    )
    grad_normed = grad_attn * gains[0] + grad_mlp * gains[2]
    row_sums = jnp.stack([jnp.sum(grad_normed, axis=1), jnp.sum(grad_normed * normed, axis=1)], axis=0)
    return normed, inv_std, branch, grad_normed, row_sums, sums, (qkvs, denses, ups, downs), db_qkv, db_up


def by_part(weight, heads):
    rows = weight.shape[0]
    return weight.reshape(rows, heads, 3, HD).transpose(0, 2, 1, 3).reshape(rows, -1)


def by_head(weight, heads):
    rows = weight.shape[0]
    return weight.reshape(rows, 3, heads, HD).transpose(0, 2, 1, 3).reshape(rows, -1)


BLOCK = 256
PER_US = 5 * 10**8
PARTS = LEN // BLOCK


def part_rows(part):
    return pl.ds(part * BLOCK, BLOCK)


def call(kernel, outs, args, took, scratch=(), after=()):
    moved = sum(x.size * x.dtype.itemsize for x in args) + sum(x.size * x.dtype.itemsize for x in outs)
    args, held, count = list(args), len(args), len(after)

    def body(*refs):
        kernel(*refs[:held], *refs[held + count :])

    args = args + list(after)
    return pl.pallas_call(
        body,
        out_shape=tuple(outs),
        in_specs=[pl.BlockSpec(memory_space=pltpu.VMEM)] * held + [pl.BlockSpec(memory_space=pl.ANY)] * count,
        out_specs=tuple([pl.BlockSpec(memory_space=pltpu.VMEM)] * len(outs)),
        scratch_shapes=list(scratch),
        compiler_params=pltpu.CompilerParams(vmem_limit_bytes=56 * 1024 * 1024),
        cost_estimate=pl.CostEstimate(flops=int(took * PER_US), bytes_accessed=1024, transcendentals=0),
    )(*args)


def tie(values, deps):
    values, deps = list(values), list(deps)
    anywhere = pl.BlockSpec(memory_space=pl.ANY)
    return pl.pallas_call(
        lambda *refs: None,
        out_shape=tuple(shape(value.shape, value.dtype) for value in values),
        in_specs=[anywhere] * (len(values) + len(deps)),
        out_specs=(anywhere,) * len(values),
        input_output_aliases={at: at for at in range(len(values))},
        cost_estimate=pl.CostEstimate(flops=1, bytes_accessed=1, transcendentals=0),
    )(*values, *deps)


def shape(dims, kind):
    return jax.ShapeDtypeStruct(dims, kind)


def row_stats(values):
    count = values.shape[1]
    mean = jnp.sum(values, axis=1, keepdims=True) * (1.0 / count)
    square = jnp.sum(values * values, axis=1, keepdims=True) * (1.0 / count)
    return mean, lax.rsqrt(square - mean * mean + EPS)


def joined_rows(mine, other, rows):
    return jnp.concatenate([part[rows, :] for pair in zip(mine, other) for part in pair], axis=1)


def grad_kernel(*refs):
    mine, other, (g_ref, gt_ref, sum_ref) = refs[:4], refs[4:8], refs[8:]
    total = jnp.zeros(sum_ref.shape, F32)
    for part in range(PARTS):
        rows = part_rows(part)
        value = joined_rows(mine, other, rows)
        wide = value.astype(F32)
        g_ref[rows, :] = value
        gt_ref[:, rows] = wide.T.astype(BF16)
        total = total + jnp.sum(wide, axis=0, keepdims=True)
    sum_ref[...] = total


def norm_kernel(*refs):
    mine, other, vec_ref, (a_ref, at_ref, m_ref, mt_ref) = refs[:4], refs[4:8], refs[8], refs[9:]
    for part in range(PARTS):
        rows = part_rows(part)
        value = joined_rows(mine, other, rows).astype(F32)
        mean, inv_std = row_stats(value)
        normed = (value - mean) * inv_std
        attn = normed * vec_ref[0:1, :] + vec_ref[1:2, :]
        a_ref[rows, :] = attn.astype(BF16)
        at_ref[:, rows] = attn.T.astype(BF16)
        mlp = normed * vec_ref[2:3, :] + vec_ref[3:4, :]
        m_ref[rows, :] = mlp.astype(BF16)
        mt_ref[:, rows] = mlp.T.astype(BF16)


def attention_box_kernel(width, count, x_ref, xt_ref, g_ref, gt_ref, keep_ref, up_ref, down_ref, *refs):
    packs, biases, refs = refs[:count], refs[count : 2 * count], refs[2 * count :]
    outs, scratch = refs[: 4 * count], refs[4 * count :]
    for at in range(count):
        heads_ref, dqkv_ref, db_ref, dw_ref = outs[4 * at : 4 * at + 4]
        pack_ref = packs[at]
        attention_kernel(
            width, x_ref, pack_ref.at[:, : 3 * width], biases[at], g_ref, pack_ref.at[:, 3 * width :], keep_ref,
            up_ref, down_ref, heads_ref, dqkv_ref, db_ref, *scratch,
        )
        for part in range(PARTS):
            rows = part_rows(part)
            dw_ref[rows, : 3 * width] = mm(xt_ref[rows, :], dqkv_ref[...]).astype(BF16)
            dw_ref[rows, 3 * width :] = mm(gt_ref[rows, :], heads_ref[...]).astype(BF16)


def attention_box(attn_in, attn_t, packs, biases, grad, grad_t, tables, after):
    width = packs[0].shape[1] // 4
    features = attn_in.shape[1]
    count = len(packs)
    square = pltpu.VMEM((LEN, width), BF16)
    turned = pltpu.VMEM((width, LEN), BF16)
    sums = pltpu.VMEM((LEN, width), F32)
    out = [shape((LEN, width), BF16), shape((LEN, 3 * width), BF16), shape((1, 3 * width), F32), shape(packs[0].shape, BF16)]
    outs = call(
        functools.partial(attention_box_kernel, width, count),
        out * count,
        [attn_in, attn_t, grad, grad_t, *tables, *packs, *biases],
        took=11 * count,
        scratch=[square] * 4 + [turned] * 2 + [sums] * 2,
        after=after,
    )
    return [outs[4 * at : 4 * at + 4] for at in range(count)]


def feed_box_kernel(count, x_ref, xt_ref, g_ref, gt_ref, *refs):
    ups, downs, biases, outs = refs[:count], refs[count : 2 * count], refs[2 * count : 3 * count], refs[3 * count :]
    for at in range(count):
        act_ref, dpre_ref, db_ref, dup_ref, ddown_ref = outs[5 * at : 5 * at + 5]
        total = jnp.zeros(db_ref.shape, F32)
        bias = biases[at][...]
        for part in range(PARTS):
            rows = part_rows(part)
            pre = mm(x_ref[rows, :], ups[at][...]) + bias
            grad_act = mm(g_ref[rows, :], downs[at][...])
            phi = 0.5 + 0.5 * lax.erf(pre * (0.5 ** 0.5))
            slope = phi + pre * (jnp.exp(-0.5 * pre * pre) * 0.3989422804014327)
            act_ref[rows, :] = (pre * phi).astype(BF16)
            dpre = (slope * grad_act).astype(BF16)
            dpre_ref[rows, :] = dpre
            total = total + jnp.sum(dpre.astype(F32), axis=0, keepdims=True)
        db_ref[...] = total
        for part in range(PARTS):
            rows = part_rows(part)
            dup_ref[rows, :] = mm(xt_ref[rows, :], dpre_ref[...]).astype(BF16)
            ddown_ref[rows, :] = mm(gt_ref[rows, :], act_ref[...]).astype(BF16)


def feed_box(mlp_in, mlp_t, ups, downs, biases, grad, grad_t, after):
    columns = ups[0].shape[1]
    features = mlp_in.shape[1]
    count = len(ups)
    out = [shape((LEN, columns), BF16)] * 2 + [shape((1, columns), F32)] + [shape(ups[0].shape, BF16)] * 2
    outs = call(
        functools.partial(feed_box_kernel, count),
        out * count,
        [mlp_in, mlp_t, grad, grad_t, *ups, *downs, *biases],
        took=7 * count,
        after=after,
    )
    return [outs[5 * at : 5 * at + 5] for at in range(count)]


def out_kernel(half, *refs):
    heads, acts, apacks, downs, (keep_ref, send_ref) = refs[:4], refs[4:8], refs[8:12], refs[12:16], refs[16:]
    width = heads[0].shape[1]
    for part in range(PARTS):
        rows = part_rows(part)
        total = None
        for k in range(4):
            term = mm_t(acts[k][rows, :], downs[k][...]) + mm_t(heads[k][rows, :], apacks[k][:, 3 * width :])
            total = term if total is None else total + term
        for k in range(4):
            to = slice(k * half, (k + 1) * half)
            keep_ref[rows, to] = total[:, 2 * k * half : (2 * k + 1) * half]
            send_ref[rows, to] = total[:, (2 * k + 1) * half : (2 * k + 2) * half].astype(BF16)


def in_kernel(half, *refs):
    mine, other, vec_ref = refs[:4], refs[4:8], refs[8]
    dqkvs, dpres, apacks, ups = refs[9:13], refs[13:17], refs[17:21], refs[21:25]
    keep_ref, send_ref, row_ref, sum_ref = refs[25:]
    width3 = dqkvs[0].shape[1]
    lane = lax.broadcasted_iota(jnp.int32, (BLOCK, 128), 1)
    sums = [jnp.zeros((1, sum_ref.shape[1]), F32) for _ in range(4)]
    for part in range(PARTS):
        rows = part_rows(part)
        grad_attn = grad_mlp = None
        for k in range(4):
            first = mm_t(dqkvs[k][rows, :], apacks[k][:, :width3])
            second = mm_t(dpres[k][rows, :], ups[k][...])
            grad_attn = first if k == 0 else grad_attn + first
            grad_mlp = second if k == 0 else grad_mlp + second
        value = joined_rows(mine, other, rows).astype(F32)
        mean, inv_std = row_stats(value)
        normed = (value - mean) * inv_std
        for at, term in enumerate((grad_attn * normed, grad_attn, grad_mlp * normed, grad_mlp)):
            sums[at] = sums[at] + jnp.sum(term, axis=0, keepdims=True)
        total = grad_attn * vec_ref[0:1, :] + grad_mlp * vec_ref[2:3, :]
        plain = jnp.sum(total, axis=1, keepdims=True)
        cross = jnp.sum(total * normed, axis=1, keepdims=True)
        both = jnp.where(lane == 0, plain, jnp.where(lane == 1, cross, 0.0))
        row_ref[:, rows] = both.T[:8, :]
        for k in range(4):
            to = slice(k * half, (k + 1) * half)
            keep_ref[rows, to] = total[:, 2 * k * half : (2 * k + 1) * half]
            send_ref[rows, to] = total[:, (2 * k + 1) * half : (2 * k + 2) * half].astype(BF16)
    for at in range(4):
        sum_ref[at : at + 1, :] = sums[at]


def final_kernel(features, half, *refs):
    mine, other, grads = refs[:4], refs[4:8], refs[8:12]
    keep_ref, got_ref, row_ref = refs[12:15]
    outs = refs[15:]
    for part in range(PARTS):
        rows = part_rows(part)
        mean, inv_std = row_stats(joined_rows(mine, other, rows).astype(F32))
        padded = jnp.concatenate([row_ref[:, rows], jnp.zeros((120, BLOCK), F32)], axis=0).T
        plain = padded[:, 0:1] * (1.0 / features)
        cross = padded[:, 1:2] * (1.0 / features)
        for k in range(4):
            to = slice(k * half, (k + 1) * half)
            total = keep_ref[rows, to] + got_ref[rows, to].astype(F32)
            normed = (mine[k][rows, :].astype(F32) - mean) * inv_std
            outs[k][rows, :] = (grads[k][rows, :].astype(F32) + inv_std * (total - plain - normed * cross)).astype(BF16)


def weights_kernel(heads, place_ref, *refs):
    att, ups, downs, (qkv_ref, dense_ref, up_ref, down_ref) = refs[:4], refs[4:8], refs[8:12], refs[12:]
    dp, gx = place_ref[0], place_ref[1]
    width, columns = att[0].shape[1] // 4, ups[0].shape[1]
    half = att[0].shape[0] // 2
    for k in range(4):
        quarter = dp ^ k
        for part in range(2):
            rows = pl.ds(part * half, half)
            to = pl.ds(pl.multiple_of((gx ^ part) * half, half), half)
            value = att[k][rows, :].astype(F32)
            pieces = [
                value[:, kind * width + head * HD : kind * width + (head + 1) * HD]
                for head in range(heads) for kind in range(3)
            ]
            qkv_ref[to, pl.ds(pl.multiple_of(quarter * 3 * width, 128), 3 * width)] = jnp.concatenate(pieces, axis=1)
            dense_ref[pl.ds(pl.multiple_of(quarter * width, 128), width), to] = value[:, 3 * width :].T
            up_ref[to, pl.ds(pl.multiple_of(quarter * columns, 128), columns)] = ups[k][rows, :].astype(F32)
            down_ref[pl.ds(pl.multiple_of(quarter * columns, 128), columns), to] = downs[k][rows, :].astype(F32).T


def local_box(
    hidden_in, ln1_gain, ln1_bias, ln2_gain, ln2_bias, w_qkv, b_qkv, w_dense, b_dense, w_up, b_up,
    w_down, b_down, cotangent,
):
    dp, gx, gy = lax.axis_index("dp"), lax.axis_index("gx"), lax.axis_index("gy")
    wide = hidden_in.shape[1]
    features = 4 * wide
    half = wide // 2
    lower = gx == 0
    aligned = (gy // 2) == gx
    odd = (gy % 2) == 1

    def rel_rows(value):
        return jnp.where(lower, value, jnp.roll(value, -half, axis=0))

    def cut_half(value):
        value = value.reshape(2, LEN, wide)
        first, second = value[:, :, :half], value[:, :, half:]
        return jnp.where(lower, first, second), jnp.where(lower, second, first)

    def pieces_of(kept, got):
        near = jnp.where(aligned, kept, got)
        far = jnp.where(aligned, got, kept)
        return [
            jnp.where(odd, near[1], near[0]), jnp.where(odd, near[0], near[1]),
            jnp.where(odd, far[1], far[0]), jnp.where(odd, far[0], far[1]),
        ]

    def exchange_z(pieces, deps):
        if deps:
            pieces = [pieces[0]] + list(tie(pieces[1:], deps))
        return [pieces[0]] + [swap(pieces[k], "gy", k, 4) for k in (1, 2, 3)]

    def from_half(got):
        near = jnp.stack([jnp.where(odd, got[1], got[0]), jnp.where(odd, got[0], got[1])])
        far = jnp.stack([jnp.where(odd, got[3], got[2]), jnp.where(odd, got[2], got[3])])
        own = jnp.where(aligned, near, far)
        back = swap(jnp.where(aligned, far, near), "gx", 1, 2)
        first = jnp.where(lower, own, back)
        second = jnp.where(lower, back, own)
        return jnp.concatenate([first, second], axis=2).reshape(2 * LEN, wide)

    heads = w_qkv.shape[1] // (3 * HD) // 4

    def columns_of(value):
        return lax.dynamic_slice_in_dim(value, dp * (value.shape[1] // 4), value.shape[1] // 4, 1)

    def rows_of(value):
        return lax.dynamic_slice_in_dim(value, dp * (value.shape[0] // 4), value.shape[0] // 4, 0).T

    def gather_z(value, deps=()):
        sent = tie([value], deps)[0] if deps else value
        return [sent] + [swap(sent, "gy", k, 4) for k in (1, 2, 3)]

    def spread(value):
        block = jnp.concatenate(value, axis=0)
        core = swap(block, "dp", 1, 4)
        across = swap(block, "dp", 2, 4)
        return [block, core, across, swap(across, "dp", 1, 4)]

    att_z = gather_z(rel_rows(jnp.concatenate([by_part(columns_of(w_qkv), heads), rows_of(w_dense)], axis=1)))
    vectors = rel_rows(jnp.stack([ln1_gain, ln1_bias, ln2_gain, ln2_bias, b_dense + b_down]).T).T
    vectors = jnp.concatenate(gather_z(vectors), axis=1)
    up_own, down_own = rel_rows(columns_of(w_up)), rel_rows(rows_of(w_down))
    hidden_kept, hidden_sent = cut_half(hidden_in)
    hidden_got = swap(hidden_sent, "gx", 1, 2)
    grad_kept, grad_sent = cut_half(cotangent)
    grad_got = swap(tie([grad_sent], [hidden_got])[0], "gx", 1, 2)
    hidden_half = exchange_z(pieces_of(hidden_kept, hidden_got), att_z[1:])
    hidden_other = [swap(piece, "gx", 1, 2) for piece in hidden_half]
    att_packs = spread(att_z)
    grad_half = exchange_z(pieces_of(grad_kept, grad_got), hidden_half[1:] + [att_packs[1]])
    grad_other = [swap(piece, "gx", 1, 2) for piece in grad_half]

    square = shape((LEN, features), BF16)
    attn_in, attn_t, mlp_in, mlp_t = call(
        norm_kernel, [square] * 4, [*hidden_half, *hidden_other, vectors], took=4
    )
    up_z = gather_z(up_own, grad_half[1:] + hidden_other[1:] + att_packs[2:3])
    ups = spread(up_z)
    b_qkv_c = xor_order(by_part(b_qkv.reshape(4, -1), heads), dp, 4)
    b_up_c = xor_order(b_up.reshape(4, -1), dp, 4)

    grad, grad_t, grad_sum = call(
        grad_kernel, [square, square, shape((1, features), F32)], [*grad_half, *grad_other], took=2,
        after=[attn_in],
    )
    down_z = gather_z(down_own, up_z[1:] + [grad])
    downs = spread(down_z)
    tables = rope_tables(att_packs[0].shape[1] // 4)

    mixed, dqkv, db_qkv, acts, dpre, db_up, att_sums, up_sums, down_sums = [[None] * 4 for _ in range(9)]

    def attention(pair, after):
        outs = attention_box(
            attn_in, attn_t, [att_packs[k] for k in pair], [b_qkv_c[k : k + 1] for k in pair], grad, grad_t, tables, after
        )
        for k, out in zip(pair, outs):
            mixed[k], dqkv[k], db_qkv[k], att_sums[k] = out

    def feed(pair, after):
        outs = feed_box(
            mlp_in, mlp_t, [ups[k] for k in pair], [downs[k] for k in pair], [b_up_c[k : k + 1] for k in pair], grad,
            grad_t, after,
        )
        for k, out in zip(pair, outs):
            acts[k], dpre[k], db_up[k], up_sums[k], down_sums[k] = out

    def far_sum(sums):
        return (sums[2].astype(F32) + swap(sums[3], "dp", 1, 4).astype(F32)).astype(BF16)

    def whole_sum(sums, far):
        total = sums[0].astype(F32) + swap(sums[1], "dp", 1, 4).astype(F32) + far.astype(F32)
        blocks = total.reshape(4, wide, -1)
        low = blocks[1:].astype(BF16)
        return blocks[0], [low[0], low[1], low[2]]

    def sum_z(blocks, deps):
        got = exchange_z([None] + blocks[1], deps)
        return blocks[0], got[1:]

    def quarters(own, got):
        mine = (own + got[0].astype(F32) + got[1].astype(F32) + got[2].astype(F32)).astype(BF16)
        return [mine] + [swap(mine, "dp", k, 4) for k in (1, 2, 3)]

    attention((3, 2), [])
    att_far = far_sum(att_sums)
    attention((1, 0), down_z[1:] + [ups[2], att_far])
    att_far_got = swap(att_far, "dp", 2, 4)
    feed((3, 2), [mixed[0], att_far_got])
    att_sum = whole_sum(att_sums, att_far_got)
    up_far, down_far = far_sum(up_sums), far_sum(down_sums)
    feed((1, 0), [acts[2], up_far, down_far] + att_sum[1])
    att_own, att_got = sum_z(att_sum, [])
    up_far_got = swap(up_far, "dp", 2, 4)
    down_far_got = swap(tie([down_far], [up_far_got])[0], "dp", 2, 4)
    up_sum = whole_sum(up_sums, up_far_got)

    keep, send = call(
        functools.partial(out_kernel, half),
        [shape((LEN, 4 * half), F32), shape((LEN, 4 * half), BF16)],
        [*mixed, *acts, *att_packs, *downs],
        took=10,
    )
    out_send = send
    got = swap(send, "gx", 1, 2)
    out_half = [
        (
            hidden_half[k].astype(F32)
            + keep[:, k * half : (k + 1) * half]
            + got[:, k * half : (k + 1) * half].astype(F32)
            + vectors[4:5, 2 * k * half : (2 * k + 1) * half]
        ).astype(BF16)
        for k in range(4)
    ]
    up_own, up_got = sum_z(up_sum, att_got)
    down_sum = whole_sum(down_sums, down_far_got)
    down_own, down_got = sum_z(down_sum, up_got)
    out_z = exchange_z(out_half, down_got)
    hidden_out = from_half(out_z)

    keep, send, row_sums, sums = call(
        functools.partial(in_kernel, half),
        [shape((LEN, 4 * half), F32), shape((LEN, 4 * half), BF16), shape((8, LEN), F32), shape((4, features), F32)],
        [*hidden_half, *hidden_other, vectors, *dqkv, *dpre, *att_packs, *ups],
        took=15,
        after=[out_send] + up_got + down_sum[1],
    )
    got = swap(send, "gx", 1, 2)
    row_sums = row_sums + swap(row_sums, "gx", 1, 2)
    in_half = call(
        functools.partial(final_kernel, features, half),
        [shape((LEN, half), BF16)] * 4,
        [*hidden_half, *hidden_other, *grad_half, keep, got, row_sums],
        took=3,
    )
    grad_input = from_half(exchange_z(list(in_half), out_z[1:]))
    att_grads, up_grads = quarters(att_own, att_got), quarters(up_own, up_got)
    down_grads = quarters(down_own, down_got)

    sums = jnp.concatenate([sums, 0.5 * grad_sum], axis=0).reshape(5, 4, 2, half)
    sums = xor_order(xor_order(sums.transpose(1, 0, 2, 3), gy, 4).transpose(2, 0, 1, 3), gx, 2)
    db_qkv = by_head(jnp.concatenate(db_qkv, axis=0), heads)
    db = xor_order(jnp.concatenate([db_qkv, jnp.concatenate(db_up, axis=0)], axis=1), dp, 4).reshape(1, -1)
    db = jnp.concatenate([db, jnp.zeros_like(db)], axis=0)
    db = jnp.where(lower, db, db[::-1])
    both = jnp.concatenate([sums.reshape(-1, 128), db.reshape(-1, 128)], axis=0)
    for axis, step, count in (("dp", 1, 4), ("dp", 2, 4), ("gx", 1, 2), ("gy", 1, 4), ("gy", 2, 4)):
        both = both + swap(both, axis, step, count)
    split = sums.size // 128
    sums = both[:split].reshape(2, 4, 5, half)
    mine = lax.dynamic_index_in_dim(sums, gy, 1, keepdims=False).transpose(1, 0, 2).reshape(5, wide)
    db = lax.dynamic_index_in_dim(both[split:].reshape(2, 4, -1), gx, 0, keepdims=False)
    columns = db_qkv.shape[1]

    place = jnp.stack([dp, gx]).astype(jnp.int32)
    vmem = pl.BlockSpec(memory_space=pltpu.VMEM)
    grad_w_qkv, grad_w_dense, grad_w_up, grad_w_down = pl.pallas_call(
        functools.partial(weights_kernel, heads),
        out_shape=tuple(shape(value.shape, F32) for value in (w_qkv, w_dense, w_up, w_down)),
        in_specs=[pl.BlockSpec(memory_space=pltpu.SMEM)] + [vmem] * 12,
        out_specs=(vmem,) * 4,
        compiler_params=pltpu.CompilerParams(vmem_limit_bytes=24 * 1024 * 1024),
    )(place, *att_grads, *up_grads, *down_grads)
    return (
        hidden_out, grad_input, mine[0], mine[1], mine[2], mine[3], grad_w_qkv, db[:, :columns].reshape(-1),
        grad_w_dense, mine[4], grad_w_up, db[:, columns:].reshape(-1), grad_w_down, mine[4],
    )


def local_any(
    gx_count, gy_count,
    hidden_in, ln1_gain, ln1_bias, ln2_gain, ln2_bias, w_qkv, b_qkv, w_dense, b_dense, w_up, b_up,
    w_down, b_down, cotangent,
):
    heads = w_qkv.shape[1] // (3 * HD)

    def to_sequence(value):
        rows = lax.all_gather(value, "gx", axis=0, tiled=True)
        return lax.all_to_all(rows, "gy", split_axis=0, concat_axis=1, tiled=True)

    def from_sequence(value):
        return lax.all_to_all(value, "gy", split_axis=1, concat_axis=0, tiled=True)

    def gather(value):
        return lax.all_gather(value, "gy", axis=0, tiled=True)

    hidden, grad = to_sequence(hidden_in), to_sequence(cotangent)
    vectors = jnp.stack([ln1_gain, ln1_bias, ln2_gain, ln2_bias])
    vectors = lax.all_gather(vectors, "gy", axis=1, tiled=True)
    chunk = (
        gather(by_part(w_qkv, heads)),
        by_part(b_qkv[None], heads)[0],
        gather(w_dense.T),
        gather(w_up),
        b_up,
        gather(w_down.T),
    )

    def reduce_chunk(grads):
        return lax.psum(lax.psum_scatter(grads[0], "gy", scatter_dimension=0, tiled=True), "dp")

    normed, inv_std, branch, grad_normed, row_sums, sums, reduced, db_qkv, db_up = sequence_pass(
        hidden, grad, vectors, [chunk], reduce_chunk
    )
    branch_rows = lax.psum_scatter(from_sequence(branch), "gx", scatter_dimension=0, tiled=True)
    hidden_out = (hidden_in.astype(F32) + branch_rows + b_dense + b_down).astype(BF16)
    features = normed.shape[1]
    row_sums = lax.psum(row_sums, "gx")
    grad_normed = grad_normed - (
        row_sums[0][:, None] / features + normed * (row_sums[1][:, None] / features)
    ) * (1.0 / gx_count)
    grad_rows = lax.psum_scatter(from_sequence(inv_std * grad_normed), "gx", scatter_dimension=0, tiled=True)
    grad_input = (cotangent.astype(F32) + grad_rows).astype(BF16)
    sums = lax.psum_scatter(sums, "gy", scatter_dimension=1, tiled=True)
    sums = lax.psum(sums * jnp.array([1.0] * 4 + [1.0 / gx_count], F32)[:, None], ("dp", "gx"))
    db_qkv, db_up = lax.psum((by_head(db_qkv, heads)[0], db_up[0]), ("dp", "gy"))
    qkvs, denses, ups, downs = reduced
    return (
        hidden_out, grad_input, sums[0], sums[1], sums[2], sums[3], by_head(qkvs, heads), db_qkv,
        denses.T, sums[4], ups, db_up, downs.T, sums[4],
    )


def solution(mesh):
    sizes = mesh.shape
    boxed = sizes["dp"] == 4 and sizes["gx"] == 2 and sizes["gy"] == 4
    rows, feature = P(("dp", "gx"), "gy"), P("gy")
    placed = (
        rows, feature, feature, feature, feature, P("gy", "gx"), P("gx"), P("gx", "gy"), feature,
        P("gy", "gx"), P("gx"), P("gx", "gy"), feature, rows,
    )
    return jax.shard_map(
        local_box if boxed else functools.partial(local_any, sizes["gx"], sizes["gy"]),
        mesh=mesh,
        in_specs=placed,
        out_specs=(rows, rows) + placed[1:5] + placed[5:13],
        check_vma=False,
    )
```
